32 devices in a mesh: groups: 2 (over x), narrow: 16 (over z, y, core).
Axes of the slice: x: 2, y: 2, z: 4, core: 2. Of those that a mesh axis runs over, the one named last changes fastest.
Arguments:
- modes: bfloat16 [32768, 1024], P(('groups', 'narrow')), parts along dimension 0, may hold values from -6 to 6
- node_index: int32 [3, 65536], P(None, ('groups', 'narrow')), parts along dimension 1, may hold values from 0 to 16383, as said below
- interp_weight: float32 [3, 65536], P(None, ('groups', 'narrow')), parts along dimension 1, may hold values from 0.1 to 1
- leaf_order: int32 [65536], P(('groups', 'narrow')), parts along dimension 0, may hold values from 0 to 2047, as said below
- leaf_inverse: bfloat16 [65536, 2048], P(('groups', 'narrow')), parts along dimension 0
- v_factor: float32 [4, 64, 65536], P(None, None, ('groups', 'narrow')), parts along dimension 2
- u_factor: float32 [4, 64, 65536], P(None, None, ('groups', 'narrow')), parts along dimension 2, may hold values from -0.375 to 0.375
- core_table: float32 [30, 128, 128], P('groups'), parts along dimension 0
- level_rank: int32 [8], P('groups'), parts along dimension 0, may hold values from 16 to 64, as said below
Outputs:
- potential: float32 [65536, 1024], P(('groups', 'narrow')), parts along dimension 0
The draws below stay inside these ranges and needn't reach their ends.
There are 2 independent parts, one for each index of `groups`. The reference program is written for one: setup_inputs(seed, part) draws one part's arguments, and reference() takes and returns one part's arrays. A program takes and returns all parts, laid end to end along the dimension named above; each array names one. Nothing has to cross between parts.
Inputs may be any that keep to these rules, and one draw needn't show every extreme that they name: node_index[j, p] lies between (p // 2048) * 1024 - 128 and (p // 2048 + 1) * 1024 + 127, clipped to the nodes that exist; both ends are reached in every leaf. `leaf_order`: each aligned block of 2048 entries is a permutation of 0 to 2047. `level_rank`: some level has rank 64.
All inputs are finite; a program needn't handle non-finite values.
Results may differ from the reference program's by a relative error of at most 0.0029.
Values may be sent and summed in bfloat16 or wider, within the bound.
No kernel may reach another device: no remote copies, remote signals or barrier semaphores. Data moves between devices by JAX's collectives and lax.ppermute only.
A program may use at most 192 MiB of HBM per device.

```python
import jax
import jax.numpy as jnp
from jax import lax

LEAF = 2048
K = 64
RHS = 1024
NODE_DEV = 1024
HALO = 128
LEVELS = 4
PANELS = 32768
NODES = 16384
CORES = 15


def draw_node_index(key, part):
    key = jax.random.fold_in(key, 5)
    panel = jnp.arange(PANELS, dtype=jnp.int32)
    lowest = panel // LEAF * NODE_DEV - HALO
    offset = jax.random.randint(key, (3, PANELS), 0, NODE_DEV + 2 * HALO)
    chosen = lowest[None, :] + offset
    within = (panel % LEAF)[None, :]
    chosen = jnp.where(within == 0, lowest[None, :], chosen)
    chosen = jnp.where(within == 1, lowest[None, :] + NODE_DEV + 2 * HALO - 1, chosen)
    return jnp.clip(chosen, 0, NODES - 1).astype(jnp.int32)


def draw_leaf_order(key, part):
    key = jax.random.fold_in(key, 7)
    leaves = PANELS // LEAF
    bits = jax.random.randint(key, (leaves, LEAF), 0, 1 << 19)
    scores = bits * LEAF + jnp.arange(LEAF, dtype=jnp.int32)[None, :]
    order = jnp.argsort(scores, axis=1, stable=True)
    return order.reshape(PANELS).astype(jnp.int32)


def draw_level_rank(key, part):
    key = jax.random.fold_in(key, 9)
    first_key, second_key = jax.random.split(key)
    ranks = jax.random.randint(first_key, (LEVELS,), K // 4, K + 1)
    place = jax.random.randint(second_key, (), 0, LEVELS)
    ranks = jnp.where(jnp.arange(LEVELS) == place, K, ranks)
    return ranks.astype(jnp.int32)


def draw_leaf_inverse(key, part):
    key = jax.random.fold_in(key, 11)
    rows = jnp.arange(PANELS)[:, None] % LEAF
    cols = jnp.arange(LEAF)[None, :]
    diagonal = jnp.where(rows == cols, 1.0, 0.0).astype(jnp.float32)
    noise = jax.random.normal(key, (PANELS, LEAF), jnp.float32) * (0.6 / LEAF ** 0.5)
    return (diagonal + noise).astype(jnp.bfloat16)


def draw_v_factor(key, part):
    key = jax.random.fold_in(key, 13)
    level = jnp.arange(LEVELS, dtype=jnp.float32)[:, None, None]
    scale = jnp.exp2(-0.5 * level) / LEAF ** 0.5
    noise = jax.random.normal(key, (LEVELS, K, PANELS), jnp.float32)
    return (noise * scale).astype(jnp.float32)


def draw_core_table(key, part):
    key = jax.random.fold_in(key, 17)
    eye = jnp.eye(2 * K, dtype=jnp.float32)[None, :, :]
    noise = jax.random.normal(key, (CORES, 2 * K, 2 * K), jnp.float32)
    return (eye + noise * (0.4 / (2 * K) ** 0.5)).astype(jnp.float32)


def shard_levels(stream_key, extent, cuts, low, top_value):
    factor_of, own = 1.0, jax.random.fold_in(stream_key, 6)
    for position, blocks in cuts:
        steps = jnp.exp(jax.random.uniform(jax.random.fold_in(own, position), (blocks,), jnp.float32, low / len(cuts), top_value / len(cuts)))
        factor_of = factor_of * jnp.repeat(steps, extent[position] // blocks).reshape([-1 if axis == position else 1 for axis in range(len(extent))])
    return factor_of


def centred(stream_key, extent, width, reach, pieces=(), held_as=jnp.bfloat16):
    level = shard_levels(stream_key, extent, pieces, -0.22, 0.18) if pieces else 1.0
    entries = jax.random.normal(stream_key, extent, jnp.float32) * width * level
    return jnp.minimum(jnp.maximum(entries, -reach), reach).astype(held_as)


def setup_inputs(seed: int = 0, part: int = 0) -> dict:
    splits = jax.random.split(jax.random.key(seed), 10)
    part_splits = jax.random.split(jax.random.fold_in(splits[9], part), 10)
    return {
        "modes": centred(part_splits[0], (NODES, RHS), 1.0, 6.0, ((0, 16),)),
        "node_index": draw_node_index(jax.random.fold_in(jax.random.fold_in(splits[9], part), 71), part),
        "interp_weight": jnp.clip(0.1 + 0.9 * jax.random.uniform(part_splits[2], (3, PANELS), jnp.float32) ** shard_levels(part_splits[2], (3, PANELS), ((1, 16),), -0.2, 0.2), 0.1, 1.0),
        "leaf_order": draw_leaf_order(jax.random.fold_in(jax.random.fold_in(splits[9], part), 71), part),
        "leaf_inverse": draw_leaf_inverse(jax.random.fold_in(jax.random.fold_in(splits[9], part), 71), part),
        "v_factor": draw_v_factor(jax.random.fold_in(jax.random.fold_in(splits[9], part), 71), part),
        "u_factor": centred(part_splits[6], (LEVELS, K, PANELS), (4 * K) ** -0.5, 0.375, ((2, 16),), jnp.float32),
        "core_table": draw_core_table(jax.random.fold_in(jax.random.fold_in(splits[9], part), 71), part),
        "level_rank": draw_level_rank(jax.random.fold_in(jax.random.fold_in(splits[9], part), 71), part),
    }


def reference(modes, node_index, interp_weight, leaf_order, leaf_inverse, v_factor, u_factor, core_table, level_rank):
    highest = lax.Precision.HIGHEST
    modes_wide = modes.astype(jnp.float32)
    interp_rhs = interp_weight[0][:, None] * modes_wide[node_index[0]]
    interp_rhs = interp_rhs + interp_weight[1][:, None] * modes_wide[node_index[1]]
    interp_rhs = interp_rhs + interp_weight[2][:, None] * modes_wide[node_index[2]]
    leaves = PANELS // LEAF
    source_rows = (jnp.arange(PANELS, dtype=jnp.int32) // LEAF) * LEAF + leaf_order.astype(jnp.int32)
    tree_rhs = interp_rhs[source_rows].astype(jnp.bfloat16)
    rhs_blocks = tree_rhs.reshape(leaves, LEAF, RHS)
    inverse_blocks = leaf_inverse.reshape(leaves, LEAF, LEAF)
    solved = lax.map(lambda pair: jnp.dot(pair[0], pair[1], preferred_element_type=jnp.float32), (inverse_blocks, rhs_blocks))
    level_field = solved.reshape(PANELS, RHS)
    rank_mask = (jnp.arange(K, dtype=jnp.int32)[None, :] < level_rank[:, None]).astype(jnp.float32)
    for level in range(LEVELS):
        span = LEAF * 2 ** level
        children = PANELS // span
        nodes_here = children // 2
        field_blocks = level_field.reshape(children, span, RHS)
        v_blocks = v_factor[level].reshape(K, children, span)
        proj = jnp.einsum('kci,ciq->ckq', v_blocks, field_blocks, precision=highest)
        proj = proj * rank_mask[level][None, :, None]
        stacked = proj.reshape(nodes_here, 2 * K, RHS)
        first = 2 ** (LEVELS - 1 - level) - 1
        cores = core_table[first:first + nodes_here]
        coef = jnp.einsum('nab,nbq->naq', cores, stacked, precision=highest).reshape(nodes_here, 2, K, RHS)
        coef = coef[:, ::-1].reshape(children, K, RHS) * rank_mask[level][None, :, None]
        u_blocks = u_factor[level].reshape(K, children, span)
        update = jnp.einsum('kci,ckq->ciq', u_blocks, coef, precision=highest)
        level_field = (field_blocks - update).reshape(PANELS, RHS)
    return level_field
```

```python
import functools

import jax
import jax.numpy as jnp
from jax import lax
from jax.experimental import pallas as pl
from jax.experimental.pallas import tpu as pltpu
from jax.sharding import PartitionSpec as P

HALO = 128
LANES = 128
F32 = jnp.float32
BF16 = jnp.bfloat16
F8 = jnp.float8_e4m3fn
LOW_SCALE = 4096.0
HIGHEST = lax.Precision.HIGHEST
MIB = 2**20


def whole():
    return pl.BlockSpec(memory_space=pltpu.VMEM)


def scalars():
    return pl.BlockSpec(memory_space=pltpu.SMEM)


def params(mib):
    return pltpu.CompilerParams(vmem_limit_bytes=mib * MIB)


def cost(flops, nbytes):
    return pl.CostEstimate(flops=int(flops), bytes_accessed=int(nbytes), transcendentals=0)


def ceil_to(value, unit):
    return -(-value // unit) * unit


def dot(a, b):
    return jnp.dot(a, b, preferred_element_type=F32)


def dot_nt(a, b):
    return lax.dot_general(a, b, (((1,), (1,)), ((), ())), preferred_element_type=F32)


def split(value):
    high = value.astype(BF16)
    return high, (value - high.astype(F32)).astype(BF16)


def masked_level(ref, rank_ref, level, rank_k):
    rows = ref[level * rank_k : (level + 1) * rank_k, :]
    place = lax.broadcasted_iota(jnp.int32, rows.shape, 0)
    return jnp.where(place < rank_ref[level], rows, 0.0)


def leaf_operators(
    rank_ref,
    base_ref,
    order_ref,
    index_ref,
    weight_ref,
    v_ref,
    u_ref,
    a_ref,
    ws_ref,
    h_ref,
    sh_ref,
    sl_ref,
    v_split,
    w_split,
    s_low,
    rows_scr,
    cols_scr,
    *,
    levels,
    rank_k,
    own,
):
    step = pl.program_id(0)
    steps = pl.num_programs(0)
    ranks = levels * rank_k
    block = a_ref.shape[1]
    groups = order_ref.shape[0]
    sub = block // LANES
    width = sh_ref.shape[1]

    @pl.when(step == 0)
    def _():
        for level in range(levels):
            high, low = split(masked_level(v_ref, rank_ref, level, rank_k))
            v_split[level * rank_k : (level + 1) * rank_k, :] = high
            v_split[ranks + level * rank_k : ranks + (level + 1) * rank_k, :] = low
        for first in range(0, groups, 8):
            order = order_ref[first : first + 8, :]
            row_of = lax.shift_right_logical(order, 7)
            lane_of = jnp.bitwise_and(order, LANES - 1)
            for quantity in range(6):
                ref = index_ref if quantity < 3 else weight_ref
                j = quantity % 3
                total = jnp.zeros((8, LANES), ref.dtype)
                for r in range(groups):
                    table = jnp.broadcast_to(ref[j : j + 1, r * LANES : (r + 1) * LANES], (8, LANES))
                    got = jnp.take_along_axis(table, lane_of, axis=1)
                    total = jnp.where(row_of == r, got, total)
                if quantity < 3:
                    node = total - base_ref[0]
                    col = jnp.where(
                        node < 0, node + (own + HALO), jnp.where(node >= own, node + HALO, node)
                    )
                    total = col.astype(F32)
                for r in range(8):
                    at = (first + r) * 8 + quantity
                    rows_scr[at : at + 1, :] = total[r : r + 1, :]
        for g in range(groups):
            rows_scr[g * 8 + 6 : g * 8 + 8, :] = jnp.zeros((2, LANES), F32)
        cols_scr[...] = rows_scr[...].T

    w = dot(v_split[...], a_ref[...])
    high, low = split(w[:ranks] + w[ranks:])
    lanes = pl.ds(pl.multiple_of(step * block, block), block)
    w_split[:ranks, lanes] = high
    w_split[ranks:, lanes] = low

    piece = 256
    for half in range(sub):
        group = step * sub + half
        turn = lax.rem(groups * 8 - group * 8, LANES)
        columns = pltpu.roll(cols_scr[...], turn, axis=1)
        index = [columns[:, j : j + 1].astype(jnp.int32) for j in range(3)]
        weight = [columns[:, 3 + j : 4 + j] for j in range(3)]
        rows = pl.ds(pl.multiple_of(group * LANES, LANES), LANES)
        for first in range(0, width, piece):
            place = lax.broadcasted_iota(jnp.int32, (LANES, piece), 1) + first
            s = jnp.where(place == index[0], weight[0], 0.0)
            s = s + jnp.where(place == index[1], weight[1], 0.0)
            s = s + jnp.where(place == index[2], weight[2], 0.0)
            high = s.astype(BF16)
            rest = s - high.astype(F32)
            sh_ref[rows, first : first + piece] = high
            s_low[rows, first : first + piece] = rest.astype(BF16)
            sl_ref[rows, first : first + piece] = (rest * LOW_SCALE).astype(F8)

    @pl.when(step == steps - 1)
    def _():
        for first in range(0, width, piece):
            part = dot(w_split[...], sh_ref[:, first : first + piece])
            part = part[:ranks] + part[ranks:]
            part = part + dot(w_split[:ranks, :], s_low[:, first : first + piece])
            high, low = split(part)
            ws_ref[:ranks, first : first + piece] = high
            ws_ref[ranks:, first : first + piece] = low
        for position, level in enumerate(range(levels - 2, -1, -1)):
            high, low = split(masked_level(u_ref, rank_ref, level, rank_k))
            part = dot_nt(v_split[...], high)
            part = part[:ranks] + part[ranks:] + dot_nt(v_split[:ranks, :], low)
            h_ref[:, position * rank_k : (position + 1) * rank_k] = part
        used = (levels - 1) * rank_k
        if used < h_ref.shape[1]:
            h_ref[:, used:] = jnp.zeros((ranks, h_ref.shape[1] - used), F32)


def projections(
    core_ref, ws_ref, modes_ref, low_ref, high_ref, h_ref, keep_ref, send_ref, halo_scr, p_scr
):
    ranks = keep_ref.shape[0]
    own = modes_ref.shape[0]
    half = modes_ref.shape[1] // 2
    halo_scr[:HALO, :] = low_ref[...]
    halo_scr[HALO:, :] = high_ref[...]
    piece = 256
    for first in range(0, 2 * half, piece):
        part = dot(ws_ref[:, :own], modes_ref[:, first : first + piece])
        part = part + dot(ws_ref[:, own:], halo_scr[:, first : first + piece])
        p_scr[:, first : first + piece] = part[:ranks] + part[ranks:]
    mine = pl.multiple_of(core_ref[0] * half, half)
    other = pl.multiple_of((1 - core_ref[0]) * half, half)
    keep_ref[:, :half] = p_scr[:, pl.ds(mine, half)]
    send_ref[:, :half] = p_scr[:, pl.ds(other, half)].astype(send_ref.dtype)
    keep_ref[:, half:] = h_ref[...]
    send_ref[:, half:] = h_ref[...].astype(send_ref.dtype)


def stage(info_ref, core_ref, mine_ref, other_ref, *refs, level, levels, rank_k, half):
    upper = jnp.full((rank_k, half), info_ref[1], jnp.int32) == 1
    mine = mine_ref[:rank_k, :half]
    other = other_ref[:rank_k, :half].astype(F32)
    stack = jnp.concatenate([jnp.where(upper, other, mine), jnp.where(upper, mine, other)], axis=0)
    coef = jnp.dot(core_ref[0], stack, precision=HIGHEST, preferred_element_type=F32)
    c_mine = jnp.where(upper, coef[:rank_k], coef[rank_k:])
    c_other = jnp.where(upper, coef[rank_k:], coef[:rank_k])
    if level < levels - 1:
        next_ref, send_ref, c_ref = refs[0], refs[1], refs[2]
        at = half + (levels - 2 - level) * rank_k
        h_mine = mine_ref[rank_k:, at : at + rank_k]
        h_other = other_ref[rank_k:, at : at + rank_k].astype(F32)
        q = mine_ref[rank_k:, :half] + other_ref[rank_k:, :half].astype(F32)
        q = q - jnp.dot(h_mine, c_mine, precision=HIGHEST, preferred_element_type=F32)
        q = q - jnp.dot(h_other, c_other, precision=HIGHEST, preferred_element_type=F32)
        next_ref[:, :half] = q
        send_ref[:, :half] = q.astype(send_ref.dtype)
        end = next_ref.shape[1]
        if end > half:
            h = mine_ref[rank_k:, half:end] + other_ref[rank_k:, half:end].astype(F32)
            next_ref[:, half:] = h
            send_ref[:, half:] = h.astype(send_ref.dtype)
        c_ref[0] = c_mine
        if level == 0:
            c_ref[1] = c_other
    else:
        before, keep_ref, send_ref = refs[: levels - 1], refs[-2], refs[-1]
        for ref_level, ref in enumerate(before):
            rows = slice(ref_level * rank_k, (ref_level + 1) * rank_k)
            keep_ref[rows, :] = ref[0]
            send_ref[rows, :] = ref[1] if ref_level == 0 else ref[0]
        rows = slice(level * rank_k, (level + 1) * rank_k)
        keep_ref[rows, :] = c_mine
        send_ref[rows, :] = c_other if level == 0 else c_mine


def interpolate(sh_ref, sl_ref, modes_ref, low_ref, high_ref, t_ref, m_scr, m8_scr):
    own = modes_ref.shape[0]

    @pl.when(pl.program_id(0) == 0)
    def _():
        m_scr[:own, :] = modes_ref[...]
        m_scr[own : own + HALO, :] = low_ref[...]
        m_scr[own + HALO :, :] = high_ref[...]
        m8_scr[...] = m_scr[...].astype(F8)

    piece = 256
    for first in range(0, t_ref.shape[1], piece):
        cols = slice(first, first + piece)
        part = dot(sh_ref[...], m_scr[:, cols])
        part = part + dot(sl_ref[...], m8_scr[:, cols]) * (1.0 / LOW_SCALE)
        t_ref[:, cols] = part.astype(BF16)


def leaf_solve(a_ref, t_ref, y_ref):
    piece = 256
    for first in range(0, t_ref.shape[1], piece):
        cols = slice(first, first + piece)
        y_ref[:, cols] = dot(a_ref[...], t_ref[:, cols])


def update(rank_ref, core_ref, u_ref, y_ref, keep_ref, got_ref, out_ref, c_scr, *, levels, rank_k):
    ranks = levels * rank_k
    half = keep_ref.shape[1]

    @pl.when(pl.program_id(0) == 0)
    def _():
        mine = pl.multiple_of(core_ref[0] * half, half)
        other = pl.multiple_of((1 - core_ref[0]) * half, half)
        for ref, at in ((keep_ref, mine), (got_ref, other)):
            high, low = split(ref[...])
            c_scr[:ranks, pl.ds(at, half)] = high
            c_scr[ranks : 2 * ranks, pl.ds(at, half)] = high
            c_scr[2 * ranks :, pl.ds(at, half)] = low

    u = jnp.concatenate(
        [masked_level(u_ref, rank_ref, level, rank_k) for level in range(levels)], axis=0
    ).T
    high, low = split(u)
    left = jnp.concatenate([high, low, high], axis=1)
    piece = 256
    for first in range(0, 2 * half, piece):
        cols = slice(first, first + piece)
        out_ref[:, cols] = y_ref[:, cols] - dot(left, c_scr[:, cols])


def local(
    modes,
    node_index,
    interp_weight,
    leaf_order,
    leaf_inverse,
    v_factor,
    u_factor,
    core_table,
    level_rank,
):
    own, rhs = modes.shape
    half = rhs // 2
    levels, rank_k, leaf = v_factor.shape
    ranks = levels * rank_k
    count = lax.axis_size("narrow")
    device = lax.axis_index("narrow").astype(jnp.int32)
    core = (device & 1).reshape(1)
    base = (device * own).reshape(1)
    width = own + 2 * HALO

    forward = [(i, i + 1) for i in range(count - 1)]
    backward = [(target, source) for source, target in forward]
    rim_low = lax.ppermute(modes[own - HALO :], "narrow", forward)
    rim_high = lax.ppermute(modes[:HALO], "narrow", backward)

    def partner(value, bit):
        return lax.ppermute(value, "narrow", [(s, s ^ (1 << bit)) for s in range(count)])

    v_rows = v_factor.reshape(ranks, leaf)
    u_rows = u_factor.reshape(ranks, leaf)

    def h_width(level):
        return ceil_to(rank_k * (levels - 1 - level), LANES)

    block = 256
    steps = leaf // block
    const = lambda i: (0, 0)
    ws, h, s_high, s_low = pl.pallas_call(
        functools.partial(leaf_operators, levels=levels, rank_k=rank_k, own=own),
        grid=(steps,),
        in_specs=[
            scalars(),
            scalars(),
            whole(),
            whole(),
            whole(),
            whole(),
            whole(),
            pl.BlockSpec((leaf, block), lambda i: (0, i)),
        ],
        out_specs=[whole(), whole(), whole(), whole()],
        out_shape=[
            jax.ShapeDtypeStruct((2 * ranks, width), BF16),
            jax.ShapeDtypeStruct((ranks, h_width(0)), F32),
            jax.ShapeDtypeStruct((leaf, width), BF16),
            jax.ShapeDtypeStruct((leaf, width), F8),
        ],
        scratch_shapes=[
            pltpu.VMEM((2 * ranks, leaf), BF16),
            pltpu.VMEM((2 * ranks, leaf), BF16),
            pltpu.VMEM((leaf, width), BF16),
            pltpu.VMEM((LANES, LANES), F32),
            pltpu.VMEM((LANES, LANES), F32),
        ],
        compiler_params=params(56),
        cost_estimate=cost(9e9, 14e6),
        name="leaf_operators",
    )(
        level_rank,
        base,
        leaf_order.reshape(leaf // LANES, LANES),
        node_index,
        interp_weight,
        v_rows,
        u_rows,
        leaf_inverse,
    )

    wide = half + h_width(0)
    mine, send = pl.pallas_call(
        projections,
        in_specs=[scalars()] + [whole()] * 5,
        out_specs=[whole(), whole()],
        out_shape=[
            jax.ShapeDtypeStruct((ranks, wide), F32),
            jax.ShapeDtypeStruct((ranks, wide), F32),
        ],
        scratch_shapes=[pltpu.VMEM((2 * HALO, rhs), BF16), pltpu.VMEM((ranks, rhs), F32)],
        compiler_params=params(24),
        cost_estimate=cost(1.4e9, 4e6),
        name="projections",
    )(core, ws, modes, rim_low, rim_high, h)

    def after(value, token):
        return lax.optimization_barrier((value, token))[0]

    def run_interpolate(first_block, blocks, token):
        return pl.pallas_call(
            interpolate,
            grid=(blocks,),
            in_specs=[
                pl.BlockSpec((block, width), lambda i: (i + first_block, 0)),
                pl.BlockSpec((block, width), lambda i: (i + first_block, 0)),
                whole(),
                whole(),
                whole(),
            ],
            out_specs=pl.BlockSpec((block, rhs), lambda i: (i, 0)),
            out_shape=jax.ShapeDtypeStruct((blocks * block, rhs), BF16),
            scratch_shapes=[pltpu.VMEM((width, rhs), BF16), pltpu.VMEM((width, rhs), F8)],
            compiler_params=params(32),
            cost_estimate=cost(4e9, 8e6),
            name="interpolate",
        )(s_high, s_low, modes, after(rim_low, token), rim_high)

    def run_leaf(tree_rhs, first_block, blocks, token):
        return pl.pallas_call(
            leaf_solve,
            grid=(blocks,),
            in_specs=[
                pl.BlockSpec((block, leaf), lambda i: (i + first_block, 0)),
                whole(),
            ],
            out_specs=pl.BlockSpec((block, rhs), lambda i: (i, 0)),
            out_shape=jax.ShapeDtypeStruct((blocks * block, rhs), F32),
            compiler_params=params(32),
            cost_estimate=cost(4.3e9, 10e6),
            name="leaf_solve",
        )(leaf_inverse, after(tree_rhs, token))

    def run_stage(level, mine, other, before):
        slot = 2 ** (levels - 1 - level) - 1 + (device >> (level + 1))
        info = jnp.stack([slot, (device >> level) & 1])
        last = level == levels - 1
        if last:
            out_shape = [jax.ShapeDtypeStruct((ranks, half), F32)] * 2
        else:
            shape = (mine.shape[0] - rank_k, half + h_width(level + 1))
            out_shape = [
                jax.ShapeDtypeStruct(shape, F32),
                jax.ShapeDtypeStruct(shape, BF16),
                jax.ShapeDtypeStruct((2 if level == 0 else 1, rank_k, half), F32),
            ]
        extra = before if last else []
        return pl.pallas_call(
            functools.partial(stage, level=level, levels=levels, rank_k=rank_k, half=half),
            grid_spec=pltpu.PrefetchScalarGridSpec(
                num_scalar_prefetch=1,
                grid=(1,),
                in_specs=[
                    pl.BlockSpec((1, 2 * rank_k, 2 * rank_k), lambda i, info: (info[0], 0, 0))
                ]
                + [whole()] * (2 + len(extra)),
                out_specs=[whole()] * len(out_shape),
            ),
            out_shape=out_shape,
            compiler_params=params(16),
            cost_estimate=cost(1e8, 1e6),
            name="stage",
        )(info, core_table, mine, other, *extra)

    half_blocks = steps // 2
    parts = {}

    def beside(position, token):
        if position == 0:
            parts["t0"] = run_interpolate(0, half_blocks, token)
            return parts["t0"]
        if position == 1:
            parts["t1"] = run_interpolate(half_blocks, half_blocks, token)
            parts["t"] = jnp.concatenate([parts["t0"], parts["t1"]], axis=0)
            return parts["t"]
        if position == 2:
            parts["y0"] = run_leaf(parts["t"], 0, half_blocks, token)
            return parts["y0"]
        if position == 3:
            parts["y1"] = run_leaf(parts["t"], half_blocks, half_blocks, token)
            return parts["y1"]
        return None

    before = []
    for level in range(levels):
        other = partner(send, level)
        token = beside(level, send)
        if token is not None:
            mine = after(mine, token)
        got = run_stage(level, mine, other, before)
        if level < levels - 1:
            mine, send = got[0], got[1]
            before.append(got[2])
    keep, send = got
    crossed = partner(send, 0)

    solved = jnp.concatenate([parts["y0"], parts["y1"]], axis=0)
    return pl.pallas_call(
        functools.partial(update, levels=levels, rank_k=rank_k),
        grid=(steps,),
        in_specs=[
            scalars(),
            scalars(),
            pl.BlockSpec((ranks, block), lambda i: (0, i)),
            pl.BlockSpec((block, rhs), lambda i: (i, 0)),
            whole(),
            whole(),
        ],
        out_specs=pl.BlockSpec((block, rhs), lambda i: (i, 0)),
        out_shape=jax.ShapeDtypeStruct((leaf, rhs), F32),
        scratch_shapes=[pltpu.VMEM((3 * ranks, rhs), BF16)],
        compiler_params=params(32),
        cost_estimate=cost(3.3e9, 18e6),
        name="update",
    )(level_rank, core, u_rows, solved, keep, crossed)


def solution(mesh):
    in_specs = (
        P(("groups", "narrow"), None),
        P(None, ("groups", "narrow")),
        P(None, ("groups", "narrow")),
        P(("groups", "narrow")),
        P(("groups", "narrow"), None),
        P(None, None, ("groups", "narrow")),
        P(None, None, ("groups", "narrow")),
        P("groups", None, None),
        P("groups"),
    )
    out_specs = P(("groups", "narrow"), None)
    return jax.shard_map(local, mesh=mesh, in_specs=in_specs, out_specs=out_specs, check_vma=False)
```

```python
import functools

import jax
import jax.numpy as jnp
from jax import lax
from jax.experimental import pallas as pl
from jax.experimental.pallas import tpu as pltpu
from jax.sharding import PartitionSpec as P

HALO = 128
LANES = 128
F32 = jnp.float32
BF16 = jnp.bfloat16
F8 = jnp.float8_e4m3fn
LOW_SCALE = 4096.0
HIGHEST = lax.Precision.HIGHEST
MIB = 2**20


def whole():
    return pl.BlockSpec(memory_space=pltpu.VMEM)


def anywhere():
    return pl.BlockSpec(memory_space=pl.ANY)


def in_hbm(value):
    return pltpu.with_memory_space_constraint(value, pltpu.HBM)


def scalars():
    return pl.BlockSpec(memory_space=pltpu.SMEM)


def params(mib):
    return pltpu.CompilerParams(vmem_limit_bytes=mib * MIB)


def cost(flops, nbytes):
    return pl.CostEstimate(flops=int(flops), bytes_accessed=int(nbytes), transcendentals=0)


def ceil_to(value, unit):
    return -(-value // unit) * unit


def dot(a, b):
    return jnp.dot(a, b, preferred_element_type=F32)


def dot_nt(a, b):
    return lax.dot_general(a, b, (((1,), (1,)), ((), ())), preferred_element_type=F32)


def split(value):
    high = value.astype(BF16)
    return high, (value - high.astype(F32)).astype(BF16)


def masked_level(ref, rank_ref, level, rank_k):
    rows = ref[level * rank_k : (level + 1) * rank_k, :]
    place = lax.broadcasted_iota(jnp.int32, rows.shape, 0)
    return jnp.where(place < rank_ref[level], rows, 0.0)


def interpolation_matrix(
    device_ref,
    rank_ref,
    order_hbm,
    index_hbm,
    weight_hbm,
    modes_ref,
    core_ref,
    v_hbm,
    a_hbm,
    sh_ref,
    sl_ref,
    s8_ref,
    up_ref,
    down_ref,
    cores_ref,
    vs_ref,
    a_ref,
    order_ref,
    index_ref,
    weight_ref,
    v_ref,
    rows_scr,
    cols_scr,
    sems,
    *,
    levels,
    rank_k,
):
    own = modes_ref.shape[0]
    groups = order_ref.shape[0]
    width = sh_ref.shape[1]
    device = device_ref[0]
    small = [
        pltpu.make_async_copy(order_hbm, order_ref, sems.at[2 + levels]),
        pltpu.make_async_copy(index_hbm, index_ref, sems.at[3 + levels]),
        pltpu.make_async_copy(weight_hbm, weight_ref, sems.at[4 + levels]),
    ]
    v_copy = pltpu.make_async_copy(v_hbm, v_ref, sems.at[5 + levels])
    cut = a_ref.shape[1]
    a_copy = pltpu.make_async_copy(a_hbm.at[:, pl.ds(0, cut)], a_ref, sems.at[6 + levels])
    copies = [
        pltpu.make_async_copy(modes_ref.at[pl.ds(own - HALO, HALO)], up_ref, sems.at[0]),
        pltpu.make_async_copy(modes_ref.at[pl.ds(0, HALO)], down_ref, sems.at[1]),
    ]
    for level in range(levels):
        slot = 2 ** (levels - 1 - level) - 1 + lax.shift_right_logical(device, level + 1)
        copies.append(
            pltpu.make_async_copy(core_ref.at[slot], cores_ref.at[level], sems.at[2 + level])
        )
    for copy in small + copies + [v_copy, a_copy]:
        copy.start()
    for copy in small:
        copy.wait()

    rows_scr[...] = jnp.zeros(rows_scr.shape, F32)
    base = device * own
    for first in range(0, groups, 8):
        order = order_ref[first : first + 8, :]
        row_of = lax.shift_right_logical(order, 7)
        lane_of = jnp.bitwise_and(order, LANES - 1)
        taken = []
        for ref in (index_ref, weight_ref):
            for j in range(3):
                total = jnp.zeros((8, LANES), ref.dtype)
                for r in range(groups):
                    table = jnp.broadcast_to(ref[j : j + 1, r * LANES : (r + 1) * LANES], (8, LANES))
                    got = jnp.take_along_axis(table, lane_of, axis=1)
                    total = jnp.where(row_of == r, got, total)
                taken.append(total)
        cols = []
        for node in taken[:3]:
            node = node - base
            cols.append(
                jnp.where(
                    node < 0, node + (own + HALO), jnp.where(node >= own, node + HALO, node)
                )
            )
        w = taken[3:]
        same = cols[2] == cols[0]
        w[0] = w[0] + jnp.where(same, w[2], 0.0)
        cols[2] = jnp.where(same, -1, cols[2])
        same = cols[2] == cols[1]
        w[1] = w[1] + jnp.where(same, w[2], 0.0)
        cols[2] = jnp.where(same, -1, cols[2])
        same = cols[1] == cols[0]
        w[0] = w[0] + jnp.where(same, w[1], 0.0)
        cols[1] = jnp.where(same, -1, cols[1])
        highs = [x.astype(BF16).astype(F32) for x in w]
        lows = [(x - high) * LOW_SCALE for x, high in zip(w, highs)]
        for quantity, value in enumerate([x.astype(F32) for x in cols] + highs + lows):
            for r in range(8):
                at = r * 16 + quantity
                rows_scr[first // 8, at : at + 1, :] = value[r : r + 1, :]
    for part in range(groups // 8):
        cols_scr[part] = rows_scr[part].T

    lane = lax.broadcasted_iota(jnp.int32, (LANES, LANES), 1).astype(jnp.int16)
    zero = jnp.zeros((LANES, LANES), BF16)

    def build(group, carry):
        part = lax.div(group, 8)
        turn = lax.rem(LANES - (group - part * 8) * 16, LANES)
        columns = pltpu.roll(cols_scr[part], turn, axis=1)

        def spread(j):
            return jnp.broadcast_to(columns[:, j : j + 1], (LANES, LANES))

        index = [spread(j).astype(jnp.int32).astype(jnp.int16) for j in range(3)]
        high = [spread(3 + j).astype(BF16) for j in range(3)]
        low = [spread(6 + j).astype(BF16) for j in range(3)]
        rows = pl.ds(pl.multiple_of(group * LANES, LANES), LANES)
        for first in range(0, width, LANES):
            s_high, s_low = zero, zero
            for j in range(3):
                here = (index[j] - jnp.int16(first)) == lane
                s_high = jnp.where(here, high[j], s_high)
                s_low = jnp.where(here, low[j], s_low)
            sh_ref[rows, first : first + LANES] = s_high
            sl_ref[rows, first : first + LANES] = s_low
            s8_ref[rows, first : first + LANES] = s_low.astype(F8)
        return carry

    lax.fori_loop(0, groups, build, 0)
    v_copy.wait()
    ranks = levels * rank_k
    for level in range(levels):
        high, low = split(masked_level(v_ref, rank_ref, level, rank_k))
        vs_ref[level * rank_k : (level + 1) * rank_k, :] = high
        vs_ref[ranks + level * rank_k : ranks + (level + 1) * rank_k, :] = low
    for copy in copies + [a_copy]:
        copy.wait()


def leaf_operators(
    rank_ref, v_split, u_hbm, a0_ref, a_hbm, w_ref, h_ref, left_ref, a1_ref, u_ref, sems, *, levels, rank_k
):
    ranks = levels * rank_k
    piece = 256
    cut = a0_ref.shape[1]
    pieces = range(0, a1_ref.shape[1], piece)
    copies = [
        pltpu.make_async_copy(
            a_hbm.at[:, pl.ds(cut + first, piece)],
            a1_ref.at[:, pl.ds(first, piece)],
            sems.at[1 + first // piece],
        )
        for first in pieces
    ]
    u_copy = pltpu.make_async_copy(u_hbm, u_ref, sems.at[0])
    for copy in copies + [u_copy]:
        copy.start()

    def product(block, at):
        w = dot(v_split[...], block)
        high, low = split(w[:ranks] + w[ranks:])
        w_ref[:ranks, at : at + piece] = high
        w_ref[ranks:, at : at + piece] = low

    for first in range(0, cut, piece):
        product(a0_ref[:, first : first + piece], first)
    for copy, first in zip(copies, pieces):
        copy.wait()
        product(a1_ref[:, first : first + piece], cut + first)
    u_copy.wait()
    for level in range(levels):
        rows = slice(level * rank_k, (level + 1) * rank_k)
        u_ref[rows, :] = masked_level(u_ref, rank_ref, level, rank_k)
    for position, level in enumerate(range(levels - 2, -1, -1)):
        high, low = split(u_ref[level * rank_k : (level + 1) * rank_k, :])
        part = dot_nt(v_split[...], high)
        part = part[:ranks] + part[ranks:] + dot_nt(v_split[:ranks, :], low)
        h_ref[:, position * rank_k : (position + 1) * rank_k] = part
    used = (levels - 1) * rank_k
    if used < h_ref.shape[1]:
        h_ref[:, used:] = jnp.zeros((ranks, h_ref.shape[1] - used), F32)
    for first in range(0, u_ref.shape[1], piece):
        rows = slice(first, first + piece)
        high, low = split(u_ref[:, rows].T)
        left_ref[rows, :ranks] = high
        left_ref[rows, ranks:] = low


def projections(
    device_ref,
    w_ref,
    sh_ref,
    sl_ref,
    modes_ref,
    low_ref,
    high_ref,
    h_ref,
    keep_ref,
    send_ref,
    m_ref,
    m8_ref,
    ws_scr,
    p_scr,
):
    ranks = keep_ref.shape[0]
    own = modes_ref.shape[0]
    half = modes_ref.shape[1] // 2
    m_ref[:own, :] = modes_ref[...]
    m_ref[own : own + HALO, :] = low_ref[...]
    m_ref[own + HALO :, :] = high_ref[...]
    m8_ref[...] = m_ref[...].astype(F8)
    piece = 256
    for first in range(0, sh_ref.shape[1], piece):
        cols = slice(first, first + piece)
        part = dot(w_ref[...], sh_ref[:, cols])
        part = part[:ranks] + part[ranks:]
        part = part + dot(w_ref[:ranks, :], sl_ref[:, cols]) * (1.0 / LOW_SCALE)
        high, low = split(part)
        ws_scr[:ranks, cols] = high
        ws_scr[ranks:, cols] = low
    for first in range(0, 2 * half, piece):
        cols = slice(first, first + piece)
        part = dot(ws_scr[...], m_ref[:, cols])
        p_scr[:, cols] = part[:ranks] + part[ranks:]
    core = jnp.bitwise_and(device_ref[0], 1)
    mine = pl.multiple_of(core * half, half)
    other = pl.multiple_of((1 - core) * half, half)
    keep_ref[:, :half] = p_scr[:, pl.ds(mine, half)]
    send_ref[:, :half] = p_scr[:, pl.ds(other, half)]
    keep_ref[:, half:] = h_ref[...]
    send_ref[:, half:] = h_ref[...]


def stage(device_ref, core_ref, mine_ref, other_ref, *refs, level, levels, rank_k, half):
    side = jnp.bitwise_and(lax.shift_right_logical(device_ref[0], level), 1)
    upper = jnp.full((rank_k, half), side, jnp.int32) == 1
    mine = mine_ref[:rank_k, :half]
    other = other_ref[:rank_k, :half].astype(F32)
    stack = jnp.concatenate([jnp.where(upper, other, mine), jnp.where(upper, mine, other)], axis=0)
    coef = jnp.dot(core_ref[level], stack, precision=HIGHEST, preferred_element_type=F32)
    c_mine = jnp.where(upper, coef[:rank_k], coef[rank_k:])
    c_other = jnp.where(upper, coef[rank_k:], coef[:rank_k])
    if level < levels - 1:
        next_ref, send_ref, c_ref = refs[0], refs[1], refs[2]
        at = half + (levels - 2 - level) * rank_k
        h_mine = mine_ref[rank_k:, at : at + rank_k]
        h_other = other_ref[rank_k:, at : at + rank_k].astype(F32)
        q = mine_ref[rank_k:, :half] + other_ref[rank_k:, :half].astype(F32)
        q = q - jnp.dot(h_mine, c_mine, precision=HIGHEST, preferred_element_type=F32)
        q = q - jnp.dot(h_other, c_other, precision=HIGHEST, preferred_element_type=F32)
        next_ref[:, :half] = q
        send_ref[:, :half] = q.astype(send_ref.dtype)
        end = next_ref.shape[1]
        if end > half:
            h = mine_ref[rank_k:, half:end] + other_ref[rank_k:, half:end].astype(F32)
            next_ref[:, half:] = h
            send_ref[:, half:] = h.astype(send_ref.dtype)
        c_ref[0] = c_mine
        if level == 0:
            c_ref[1] = c_other
    else:
        before, keep_ref, send_ref = refs[: levels - 1], refs[-2], refs[-1]
        for ref_level, ref in enumerate(before):
            rows = slice(ref_level * rank_k, (ref_level + 1) * rank_k)
            keep_ref[rows, :] = ref[0]
            send_ref[rows, :] = ref[1] if ref_level == 0 else ref[0]
        rows = slice(level * rank_k, (level + 1) * rank_k)
        keep_ref[rows, :] = c_mine
        send_ref[rows, :] = c_other if level == 0 else c_mine


def interpolate(sh_ref, s8_ref, m_ref, m8_ref, t_ref, *, start):
    block, piece = 512, 256
    for row in range(0, t_ref.shape[0], block):
        rows = slice(start + row, start + row + block)
        for first in range(0, t_ref.shape[1], piece):
            cols = slice(first, first + piece)
            part = dot(sh_ref[rows, :], m_ref[:, cols])
            part = part + dot(s8_ref[rows, :], m8_ref[:, cols]) * (1.0 / LOW_SCALE)
            t_ref[row : row + block, cols] = part.astype(BF16)


def leaf_solve(a0_ref, a1_ref, t0_ref, t1_ref, y_ref, *, start):
    block, piece = 512, 256
    for row in range(0, y_ref.shape[0], block):
        rows = slice(start + row, start + row + block)
        for first in range(0, y_ref.shape[1], piece):
            cols = slice(first, first + piece)
            part = dot(a0_ref[rows, :], t0_ref[:, cols]) + dot(a1_ref[rows, :], t1_ref[:, cols])
            y_ref[row : row + block, cols] = part


def update(device_ref, left_ref, y0_ref, y1_ref, keep_ref, got_ref, out_ref, c_scr, o_scr, sems):
    ranks, half = keep_ref.shape
    core = jnp.bitwise_and(device_ref[0], 1)
    mine = pl.multiple_of(core * half, half)
    other = pl.multiple_of((1 - core) * half, half)
    for ref, at in ((keep_ref, mine), (got_ref, other)):
        high, low = split(ref[...])
        c_scr[:ranks, pl.ds(at, half)] = high
        c_scr[ranks : 2 * ranks, pl.ds(at, half)] = high
        c_scr[2 * ranks :, pl.ds(at, half)] = low
    block, piece = 256, 256
    copies = []
    for row in range(0, o_scr.shape[0], block):
        rows = slice(row, row + block)
        if row < y0_ref.shape[0]:
            ref, at = y0_ref, row
        else:
            ref, at = y1_ref, row - y0_ref.shape[0]
        for first in range(0, 2 * half, piece):
            cols = slice(first, first + piece)
            part = dot(left_ref[rows, :], c_scr[: 2 * ranks, cols])
            part = part + dot(left_ref[rows, :ranks], c_scr[2 * ranks :, cols])
            o_scr[rows, cols] = ref[at : at + block, cols] - part
        copy = pltpu.make_async_copy(
            o_scr.at[pl.ds(row, block)], out_ref.at[pl.ds(row, block)], sems.at[row // block]
        )
        copy.start()
        copies.append(copy)
    for copy in copies:
        copy.wait()


def local(
    modes,
    node_index,
    interp_weight,
    leaf_order,
    leaf_inverse,
    v_factor,
    u_factor,
    core_table,
    level_rank,
):
    own, rhs = modes.shape
    half = rhs // 2
    levels, rank_k, leaf = v_factor.shape
    ranks = levels * rank_k
    count = lax.axis_size("narrow")
    device = lax.axis_index("narrow").astype(jnp.int32)
    device = device.reshape(1)
    width = own + 2 * HALO
    shape = pltpu.VMEM
    half_rows = leaf // 2

    def partner(value, bit):
        return lax.ppermute(value, "narrow", [(s, s ^ (1 << bit)) for s in range(count)])

    def after(value, token):
        return lax.optimization_barrier((value, token))[0]

    v_rows = v_factor.reshape(ranks, leaf)
    u_rows = u_factor.reshape(ranks, leaf)

    def h_width(level):
        return ceil_to(rank_k * (levels - 1 - level), LANES)

    groups = leaf // LANES
    s_high, s_low, s_low8, up, down, cores, v_split, a_left = pl.pallas_call(
        functools.partial(interpolation_matrix, levels=levels, rank_k=rank_k),
        in_specs=[scalars()] * 2 + [anywhere()] * 7,
        out_specs=[whole()] * 8,
        out_shape=[
            shape((leaf, width), BF16),
            shape((leaf, width), BF16),
            shape((leaf, width), F8),
            shape((HALO, rhs), BF16),
            shape((HALO, rhs), BF16),
            shape((levels, 2 * rank_k, 2 * rank_k), F32),
            shape((2 * ranks, leaf), BF16),
            shape((leaf, half_rows), BF16),
        ],
        scratch_shapes=[
            pltpu.VMEM((groups, LANES), jnp.int32),
            pltpu.VMEM((3, leaf), jnp.int32),
            pltpu.VMEM((3, leaf), F32),
            pltpu.VMEM((ranks, leaf), F32),
            pltpu.VMEM((groups // 8, LANES, LANES), F32),
            pltpu.VMEM((groups // 8, LANES, LANES), F32),
            pltpu.SemaphoreType.DMA((7 + levels,)),
        ],
        compiler_params=params(8),
        cost_estimate=cost(1e9, 14e6),
        name="interpolation_matrix",
    )(
        device,
        level_rank,
        in_hbm(leaf_order.reshape(groups, LANES)),
        in_hbm(node_index),
        in_hbm(interp_weight),
        in_hbm(modes),
        in_hbm(core_table),
        in_hbm(v_rows),
        in_hbm(leaf_inverse),
    )

    forward = [(i, i + 1) for i in range(count - 1)]
    backward = [(target, source) for source, target in forward]
    rim_low = lax.ppermute(up, "narrow", forward)
    rim_high = lax.ppermute(down, "narrow", backward)

    w, h, left, a_right = pl.pallas_call(
        functools.partial(leaf_operators, levels=levels, rank_k=rank_k),
        in_specs=[scalars(), whole(), anywhere(), whole(), anywhere()],
        out_specs=[whole()] * 4,
        out_shape=[
            shape((2 * ranks, leaf), BF16),
            shape((ranks, h_width(0)), F32),
            shape((leaf, 2 * ranks), BF16),
            shape((leaf, leaf - half_rows), BF16),
        ],
        scratch_shapes=[
            pltpu.VMEM((ranks, leaf), F32),
            pltpu.SemaphoreType.DMA((1 + (leaf - half_rows) // 256,)),
        ],
        compiler_params=params(6),
        cost_estimate=cost(5e9, 14e6),
        name="leaf_operators",
    )(level_rank, v_split, in_hbm(u_rows), a_left, in_hbm(leaf_inverse))

    wide = half + h_width(0)
    mine, send, m, m8 = pl.pallas_call(
        projections,
        in_specs=[scalars()] + [whole()] * 7,
        out_specs=[whole()] * 4,
        out_shape=[
            shape((ranks, wide), F32),
            shape((ranks, wide), F32),
            shape((width, rhs), BF16),
            shape((width, rhs), F8),
        ],
        scratch_shapes=[pltpu.VMEM((2 * ranks, width), BF16), pltpu.VMEM((ranks, rhs), F32)],
        compiler_params=params(8),
        cost_estimate=cost(5e9, 14e6),
        name="projections",
    )(device, w, s_high, s_low, modes, rim_low, rim_high, h)

    def run_interpolate(start, token):
        return pl.pallas_call(
            functools.partial(interpolate, start=start),
            in_specs=[whole()] * 4,
            out_specs=whole(),
            out_shape=shape((half_rows, rhs), BF16),
            compiler_params=params(4),
            cost_estimate=cost(4e9, 8e6),
            name="interpolate",
        )(s_high, s_low8, m, after(m8, token))

    def run_leaf(t0, t1, start, token):
        return pl.pallas_call(
            functools.partial(leaf_solve, start=start),
            in_specs=[whole()] * 4,
            out_specs=whole(),
            out_shape=shape((half_rows, rhs), F32),
            compiler_params=params(4),
            cost_estimate=cost(4.3e9, 10e6),
            name="leaf_solve",
        )(a_left, a_right, t0, after(t1, token))

    def run_stage(level, mine, other, before):
        if level == levels - 1:
            out_shape = [shape((ranks, half), F32)] * 2
            extra = before
        else:
            size = (mine.shape[0] - rank_k, half + h_width(level + 1))
            out_shape = [
                shape(size, F32),
                shape(size, BF16),
                shape((2 if level == 0 else 1, rank_k, half), F32),
            ]
            extra = []
        return pl.pallas_call(
            functools.partial(stage, level=level, levels=levels, rank_k=rank_k, half=half),
            in_specs=[scalars()] + [whole()] * (3 + len(extra)),
            out_specs=[whole()] * len(out_shape),
            out_shape=out_shape,
            compiler_params=params(6),
            cost_estimate=cost(1e8, 1e6),
            name="stage",
        )(device, cores, mine, other, *extra)

    parts = {}

    def beside(position, token):
        if position == 0:
            parts["t0"] = run_interpolate(0, token)
            return parts["t0"]
        if position == 1:
            parts["t1"] = run_interpolate(half_rows, token)
            return parts["t1"]
        if position == 2:
            parts["y0"] = run_leaf(parts["t0"], parts["t1"], 0, token)
            return parts["y0"]
        if position == 3:
            parts["y1"] = run_leaf(parts["t0"], parts["t1"], half_rows, token)
            return parts["y1"]
        return None

    before = []
    for level in range(levels):
        other = partner(send, level)
        token = beside(level, send)
        if token is not None:
            mine = after(mine, token)
        got = run_stage(level, mine, other, before)
        if level < levels - 1:
            mine, send = got[0], got[1]
            before.append(got[2])
    keep, send = got
    crossed = partner(send, 0)

    return pl.pallas_call(
        update,
        in_specs=[scalars()] + [whole()] * 5,
        out_specs=anywhere(),
        out_shape=jax.ShapeDtypeStruct((leaf, rhs), F32),
        scratch_shapes=[
            pltpu.VMEM((3 * ranks, rhs), BF16),
            pltpu.VMEM((leaf, rhs), F32),
            pltpu.SemaphoreType.DMA((leaf // 256,)),
        ],
        compiler_params=params(16),
        cost_estimate=cost(3.3e9, 18e6),
        name="update",
    )(device, left, parts["y0"], parts["y1"], keep, crossed)


def solution(mesh):
    in_specs = (
        P(("groups", "narrow"), None),
        P(None, ("groups", "narrow")),
        P(None, ("groups", "narrow")),
        P(("groups", "narrow")),
        P(("groups", "narrow"), None),
        P(None, None, ("groups", "narrow")),
        P(None, None, ("groups", "narrow")),
        P("groups", None, None),
        P("groups"),
    )
    out_specs = P(("groups", "narrow"), None)
    return jax.shard_map(local, mesh=mesh, in_specs=in_specs, out_specs=out_specs, check_vma=False)
```

```python
import functools

import jax
import jax.numpy as jnp
from jax import lax
from jax.experimental import pallas as pl
from jax.experimental.pallas import tpu as pltpu
from jax.sharding import PartitionSpec as P

HALO = 128
LANES = 128
F32 = jnp.float32
BF16 = jnp.bfloat16
F8 = jnp.float8_e4m3fn
LOW_SCALE = 4096.0
NOWHERE_BITS = 11
NOWHERE = 2**NOWHERE_BITS - 1
HIGHEST = lax.Precision.HIGHEST
MIB = 2**20


def whole():
    return pl.BlockSpec(memory_space=pltpu.VMEM)


def anywhere():
    return pl.BlockSpec(memory_space=pl.ANY)


def in_hbm(value):
    return pltpu.with_memory_space_constraint(value, pltpu.HBM)


def scalars():
    return pl.BlockSpec(memory_space=pltpu.SMEM)


def params(mib):
    return pltpu.CompilerParams(vmem_limit_bytes=mib * MIB)


def cost(flops, nbytes):
    return pl.CostEstimate(flops=int(flops), bytes_accessed=int(nbytes), transcendentals=0)


def ceil_to(value, unit):
    return -(-value // unit) * unit


def dot(a, b):
    return jnp.dot(a, b, preferred_element_type=F32)


def dot_nt(a, b):
    return lax.dot_general(a, b, (((1,), (1,)), ((), ())), preferred_element_type=F32)


def split(value):
    high = value.astype(BF16)
    return high, (value - high.astype(F32)).astype(BF16)


def masked_level(ref, rank_ref, level, rank_k):
    rows = ref[level * rank_k : (level + 1) * rank_k, :]
    place = lax.broadcasted_iota(jnp.int32, rows.shape, 0)
    return jnp.where(place < rank_ref[level], rows, 0.0)


def interpolation_matrix(
    device_ref,
    rank_ref,
    order_hbm,
    index_hbm,
    weight_hbm,
    modes_ref,
    core_ref,
    v_hbm,
    a_hbm,
    sh_ref,
    sl_ref,
    s8_ref,
    inner_ref,
    outer_ref,
    cores_ref,
    vs_ref,
    a_ref,
    order_ref,
    index_ref,
    weight_ref,
    v_ref,
    rows_scr,
    cols_scr,
    sems,
    *,
    levels,
    rank_k,
):
    own = modes_ref.shape[0]
    groups = order_ref.shape[0]
    width = sh_ref.shape[1]
    device = device_ref[0]
    odd = jnp.bitwise_and(device, 1)
    inner = pl.multiple_of((1 - odd) * (own - HALO), HALO)
    outer = pl.multiple_of(odd * (own - HALO), HALO)
    small = [
        pltpu.make_async_copy(order_hbm, order_ref, sems.at[2 + levels]),
        pltpu.make_async_copy(index_hbm, index_ref, sems.at[3 + levels]),
        pltpu.make_async_copy(weight_hbm, weight_ref, sems.at[4 + levels]),
    ]
    v_copy = pltpu.make_async_copy(v_hbm, v_ref, sems.at[5 + levels])
    cut = a_ref.shape[1]
    a_copy = pltpu.make_async_copy(a_hbm.at[:, pl.ds(0, cut)], a_ref, sems.at[6 + levels])
    copies = [
        pltpu.make_async_copy(modes_ref.at[pl.ds(inner, HALO)], inner_ref, sems.at[0]),
        pltpu.make_async_copy(modes_ref.at[pl.ds(outer, HALO)], outer_ref, sems.at[1]),
    ]
    for level in range(levels):
        slot = 2 ** (levels - 1 - level) - 1 + lax.shift_right_logical(device, level + 1)
        copies.append(
            pltpu.make_async_copy(core_ref.at[slot], cores_ref.at[level], sems.at[2 + level])
        )
    for copy in small + copies + [v_copy, a_copy]:
        copy.start()
    for copy in small:
        copy.wait()

    rows_scr[...] = jnp.zeros(rows_scr.shape, F32)
    base = device * own
    for first in range(0, groups, 8):
        order = order_ref[first : first + 8, :]
        row_of = lax.shift_right_logical(order, 7)
        lane_of = jnp.bitwise_and(order, LANES - 1)
        taken = []
        for ref in (index_ref, weight_ref):
            for j in range(3):
                total = jnp.zeros((8, LANES), ref.dtype)
                for r in range(groups):
                    table = jnp.broadcast_to(ref[j : j + 1, r * LANES : (r + 1) * LANES], (8, LANES))
                    got = jnp.take_along_axis(table, lane_of, axis=1)
                    total = jnp.where(row_of == r, got, total)
                taken.append(total)
        cols = []
        for node in taken[:3]:
            node = node - base
            cols.append(
                jnp.where(
                    node < 0, node + (own + HALO), jnp.where(node >= own, node + HALO, node)
                )
            )
        w = taken[3:]
        for keep, drop in ((0, 2), (1, 2), (0, 1)):
            same = cols[drop] == cols[keep]
            w[keep] = w[keep] + jnp.where(same, w[drop], 0.0)
            cols[drop] = jnp.where(same, NOWHERE, cols[drop])
        packed = [cols[0] + cols[1] * (NOWHERE + 1), cols[2]]
        for quantity, value in enumerate([x.astype(F32) for x in packed] + w):
            for r in range(8):
                at = (first + r) * 8 + quantity
                rows_scr[at : at + 1, :] = value[r : r + 1, :]
    cols_scr[...] = rows_scr[...].T

    lane = lax.broadcasted_iota(jnp.int32, (LANES, LANES), 1)
    zero = jnp.zeros((LANES, LANES), BF16)
    for group in range(groups):

        def spread(j):
            at = group * 8 + j
            return jnp.broadcast_to(cols_scr[:, at : at + 1], (LANES, LANES))

        both = spread(0).astype(jnp.int32)
        index = [
            jnp.bitwise_and(both, NOWHERE),
            lax.shift_right_logical(both, NOWHERE_BITS),
            spread(1).astype(jnp.int32),
        ]
        index = [i.astype(jnp.int16) for i in index]
        high, low = [], []
        for j in range(3):
            weight = spread(2 + j)
            high.append(weight.astype(BF16))
            low.append(((weight - high[j].astype(F32)) * LOW_SCALE).astype(BF16))
        rows = slice(group * LANES, (group + 1) * LANES)
        for first in range(0, width, LANES):
            place = (lane + first).astype(jnp.int16)
            s_high, s_low = zero, zero
            for j in range(3):
                here = index[j] == place
                s_high = jnp.where(here, high[j], s_high)
                s_low = jnp.where(here, low[j], s_low)
            sh_ref[rows, first : first + LANES] = s_high
            sl_ref[rows, first : first + LANES] = s_low
            s8_ref[rows, first : first + LANES] = s_low.astype(F8)
    v_copy.wait()
    ranks = levels * rank_k
    for level in range(levels):
        high, low = split(masked_level(v_ref, rank_ref, level, rank_k))
        vs_ref[level * rank_k : (level + 1) * rank_k, :] = high
        vs_ref[ranks + level * rank_k : ranks + (level + 1) * rank_k, :] = low
    for copy in copies + [a_copy]:
        copy.wait()


def leaf_operators(
    rank_ref, v_split, u_hbm, a0_ref, a_hbm, w_ref, h_ref, left_ref, a1_ref, u_ref, sems, *, levels, rank_k
):
    ranks = levels * rank_k
    piece = 256
    cut = a0_ref.shape[1]
    a_copy = pltpu.make_async_copy(a_hbm.at[:, pl.ds(cut, a1_ref.shape[1])], a1_ref, sems.at[0])
    u_copy = pltpu.make_async_copy(u_hbm, u_ref, sems.at[1])
    a_copy.start()
    u_copy.start()

    def product(block, at):
        w = dot(v_split[...], block)
        high, low = split(w[:ranks] + w[ranks:])
        w_ref[:ranks, at : at + piece] = high
        w_ref[ranks:, at : at + piece] = low

    for first in range(0, cut, piece):
        product(a0_ref[:, first : first + piece], first)
    a_copy.wait()
    for first in range(0, a1_ref.shape[1], piece):
        product(a1_ref[:, first : first + piece], cut + first)
    u_copy.wait()
    for level in range(levels):
        rows = slice(level * rank_k, (level + 1) * rank_k)
        u_ref[rows, :] = masked_level(u_ref, rank_ref, level, rank_k)
    high, low = split(u_ref[...])
    part = dot_nt(v_split[...], high)
    part = part[:ranks] + part[ranks:] + dot_nt(v_split[:ranks, :], low)
    for position, level in enumerate(range(levels - 2, -1, -1)):
        h_ref[:, position * rank_k : (position + 1) * rank_k] = part[
            :, level * rank_k : (level + 1) * rank_k
        ]
    used = (levels - 1) * rank_k
    if used < h_ref.shape[1]:
        h_ref[:, used:] = jnp.zeros((ranks, h_ref.shape[1] - used), F32)
    for first in range(0, u_ref.shape[1], piece):
        rows = slice(first, first + piece)
        high, low = split(u_ref[:, rows].T)
        left_ref[rows, :ranks] = high
        left_ref[rows, ranks:] = low


def projections(
    device_ref,
    w_ref,
    sh_ref,
    sl_ref,
    modes_ref,
    inner_ref,
    outer_ref,
    h_ref,
    keep_ref,
    send_ref,
    m_ref,
    m8_ref,
    ws_scr,
    p_scr,
):
    ranks = keep_ref.shape[0]
    own = modes_ref.shape[0]
    half = modes_ref.shape[1] // 2
    m_ref[:own, :] = modes_ref[...]
    core = jnp.bitwise_and(device_ref[0], 1)
    m_ref[pl.ds(pl.multiple_of(own + HALO - core * HALO, HALO), HALO), :] = inner_ref[...]
    m_ref[pl.ds(pl.multiple_of(own + core * HALO, HALO), HALO), :] = outer_ref[...]
    m8_ref[...] = m_ref[...].astype(F8)
    piece = 256
    for first in range(0, sh_ref.shape[1], piece):
        cols = slice(first, first + piece)
        part = dot(w_ref[...], sh_ref[:, cols])
        part = part[:ranks] + part[ranks:]
        part = part + dot(w_ref[:ranks, :], sl_ref[:, cols]) * (1.0 / LOW_SCALE)
        high, low = split(part)
        ws_scr[:ranks, cols] = high
        ws_scr[ranks:, cols] = low
    for first in range(0, 2 * half, piece):
        cols = slice(first, first + piece)
        part = dot(ws_scr[...], m_ref[:, cols])
        p_scr[:, cols] = part[:ranks] + part[ranks:]
    mine = pl.multiple_of(core * half, half)
    other = pl.multiple_of((1 - core) * half, half)
    keep_ref[:, :half] = p_scr[:, pl.ds(mine, half)]
    send_ref[:, :half] = p_scr[:, pl.ds(other, half)]
    keep_ref[:, half:] = h_ref[...]
    send_ref[:, half:] = h_ref[...]


def stage(device_ref, core_ref, mine_ref, other_ref, *refs, level, levels, rank_k, half):
    side = jnp.bitwise_and(lax.shift_right_logical(device_ref[0], level), 1)
    upper = jnp.full((rank_k, half), side, jnp.int32) == 1
    mine = mine_ref[:rank_k, :half]
    other = other_ref[:rank_k, :half].astype(F32)
    stack = jnp.concatenate([jnp.where(upper, other, mine), jnp.where(upper, mine, other)], axis=0)
    coef = jnp.dot(core_ref[level], stack, precision=HIGHEST, preferred_element_type=F32)
    c_mine = jnp.where(upper, coef[:rank_k], coef[rank_k:])
    c_other = jnp.where(upper, coef[rank_k:], coef[:rank_k])
    if level < levels - 1:
        next_ref, send_ref, c_ref = refs[0], refs[1], refs[2]
        at = half + (levels - 2 - level) * rank_k
        h_mine = mine_ref[rank_k:, at : at + rank_k]
        h_other = other_ref[rank_k:, at : at + rank_k].astype(F32)
        q = mine_ref[rank_k:, :half] + other_ref[rank_k:, :half].astype(F32)
        q = q - jnp.dot(h_mine, c_mine, precision=HIGHEST, preferred_element_type=F32)
        q = q - jnp.dot(h_other, c_other, precision=HIGHEST, preferred_element_type=F32)
        next_ref[:, :half] = q
        send_ref[:, :half] = q.astype(send_ref.dtype)
        end = next_ref.shape[1]
        if end > half:
            h = mine_ref[rank_k:, half:end] + other_ref[rank_k:, half:end].astype(F32)
            next_ref[:, half:] = h
            send_ref[:, half:] = h.astype(send_ref.dtype)
        c_ref[0] = c_mine
        if level == 0:
            c_ref[1] = c_other
    else:
        before, keep_ref, send_ref = refs[: levels - 1], refs[-2], refs[-1]
        for ref_level, ref in enumerate(before):
            rows = slice(ref_level * rank_k, (ref_level + 1) * rank_k)
            keep_ref[rows, :] = ref[0]
            send_ref[rows, :] = ref[1] if ref_level == 0 else ref[0]
        rows = slice(level * rank_k, (level + 1) * rank_k)
        keep_ref[rows, :] = c_mine
        send_ref[rows, :] = c_other if level == 0 else c_mine


def interpolate(sh_ref, s8_ref, m_ref, m8_ref, t_ref, *, start):
    block, piece = 512, 256
    for row in range(0, t_ref.shape[0], block):
        rows = slice(start + row, start + row + block)
        for first in range(0, t_ref.shape[1], piece):
            cols = slice(first, first + piece)
            part = dot(sh_ref[rows, :], m_ref[:, cols])
            part = part + dot(s8_ref[rows, :], m8_ref[:, cols]) * (1.0 / LOW_SCALE)
            t_ref[row : row + block, cols] = part.astype(BF16)


def leaf_solve(a0_ref, a1_ref, t0_ref, t1_ref, y_ref, *, start):
    block, piece = 512, 256
    cut, half = t0_ref.shape[0], a0_ref.shape[1]
    for row in range(0, y_ref.shape[0], block):
        rows = slice(start + row, start + row + block)
        for first in range(0, y_ref.shape[1], piece):
            cols = slice(first, first + piece)
            part = dot(a0_ref[rows, :cut], t0_ref[:, cols])
            if cut < half:
                part = part + dot(a0_ref[rows, cut:], t1_ref[: half - cut, cols])
            part = part + dot(a1_ref[rows, :], t1_ref[half - cut :, cols])
            y_ref[row : row + block, cols] = part


def update(device_ref, left_ref, y0_ref, y1_ref, c_ref, *refs, own_half):
    out_ref, c_scr, o_scr, sems = refs[-4:]
    ranks, half = c_ref.shape
    core = jnp.bitwise_and(device_ref[0], 1)
    at = pl.multiple_of((core if own_half else 1 - core) * half, half)
    high, low = split(c_ref[...])
    c_scr[:ranks, :] = high
    c_scr[ranks : 2 * ranks, :] = high
    c_scr[2 * ranks :, :] = low
    block, piece = 256, 256
    copies = []
    for row in range(0, o_scr.shape[0], block):
        rows = slice(row, row + block)
        if row < y0_ref.shape[0]:
            ref, begin = y0_ref, row
        else:
            ref, begin = y1_ref, row - y0_ref.shape[0]
        for first in range(0, half, piece):
            cols = slice(first, first + piece)
            part = dot(left_ref[rows, :], c_scr[: 2 * ranks, cols])
            part = part + dot(left_ref[rows, :ranks], c_scr[2 * ranks :, cols])
            solved = ref[begin : begin + block, pl.ds(pl.multiple_of(at + first, piece), piece)]
            o_scr[rows, cols] = solved - part
        copy = pltpu.make_async_copy(
            o_scr.at[pl.ds(row, block)],
            out_ref.at[pl.ds(row, block), pl.ds(at, half)],
            sems.at[row // block],
        )
        copy.start()
        copies.append(copy)
    for copy in copies:
        copy.wait()


def local(
    modes,
    node_index,
    interp_weight,
    leaf_order,
    leaf_inverse,
    v_factor,
    u_factor,
    core_table,
    level_rank,
):
    own, rhs = modes.shape
    half = rhs // 2
    levels, rank_k, leaf = v_factor.shape
    ranks = levels * rank_k
    count = lax.axis_size("narrow")
    device = lax.axis_index("narrow").astype(jnp.int32)
    device = device.reshape(1)
    width = own + 2 * HALO
    shape = pltpu.VMEM
    half_rows = leaf // 2

    def partner(value, bit):
        return lax.ppermute(value, "narrow", [(s, s ^ (1 << bit)) for s in range(count)])

    def after(value, token):
        return lax.optimization_barrier((value, token))[0]

    v_rows = v_factor.reshape(ranks, leaf)
    u_rows = u_factor.reshape(ranks, leaf)

    def h_width(level):
        return ceil_to(rank_k * (levels - 1 - level), LANES)

    groups = leaf // LANES
    s_high, s_low, s_low8, inner, outer, cores, v_split, a_left = pl.pallas_call(
        functools.partial(interpolation_matrix, levels=levels, rank_k=rank_k),
        in_specs=[scalars()] * 2 + [anywhere()] * 7,
        out_specs=[whole()] * 8,
        out_shape=[
            shape((leaf, width), BF16),
            shape((leaf, width), BF16),
            shape((leaf, width), F8),
            shape((HALO, rhs), BF16),
            shape((HALO, rhs), BF16),
            shape((levels, 2 * rank_k, 2 * rank_k), F32),
            shape((2 * ranks, leaf), BF16),
            shape((leaf, half_rows), BF16),
        ],
        scratch_shapes=[
            pltpu.VMEM((groups, LANES), jnp.int32),
            pltpu.VMEM((3, leaf), jnp.int32),
            pltpu.VMEM((3, leaf), F32),
            pltpu.VMEM((ranks, leaf), F32),
            pltpu.VMEM((groups * 8, LANES), F32),
            pltpu.VMEM((LANES, groups * 8), F32),
            pltpu.SemaphoreType.DMA((7 + levels,)),
        ],
        compiler_params=params(8),
        cost_estimate=cost(1e9, 14e6),
        name="interpolation_matrix",
    )(
        device,
        level_rank,
        in_hbm(leaf_order.reshape(groups, LANES)),
        in_hbm(node_index),
        in_hbm(interp_weight),
        in_hbm(modes),
        in_hbm(core_table),
        in_hbm(v_rows),
        in_hbm(leaf_inverse),
    )

    rim_inner = partner(inner, 0)
    swaps = [(i, i + 1) for i in range(1, count - 1, 2)]
    rim_outer = lax.ppermute(outer, "narrow", swaps + [(j, i) for i, j in swaps])

    w, h, left, a_right = pl.pallas_call(
        functools.partial(leaf_operators, levels=levels, rank_k=rank_k),
        in_specs=[scalars(), whole(), anywhere(), whole(), anywhere()],
        out_specs=[whole()] * 4,
        out_shape=[
            shape((2 * ranks, leaf), BF16),
            shape((ranks, h_width(0)), F32),
            shape((leaf, 2 * ranks), BF16),
            shape((leaf, leaf - half_rows), BF16),
        ],
        scratch_shapes=[
            pltpu.VMEM((ranks, leaf), F32),
            pltpu.SemaphoreType.DMA((2,)),
        ],
        compiler_params=params(10),
        cost_estimate=cost(5e9, 14e6),
        name="leaf_operators",
    )(level_rank, v_split, in_hbm(u_rows), a_left, in_hbm(leaf_inverse))

    wide = half + h_width(0)
    mine, send, m, m8 = pl.pallas_call(
        projections,
        in_specs=[scalars()] + [whole()] * 7,
        out_specs=[whole()] * 4,
        out_shape=[
            shape((ranks, wide), F32),
            shape((ranks, wide), F32),
            shape((width, rhs), BF16),
            shape((width, rhs), F8),
        ],
        scratch_shapes=[pltpu.VMEM((2 * ranks, width), BF16), pltpu.VMEM((ranks, rhs), F32)],
        compiler_params=params(8),
        cost_estimate=cost(5e9, 14e6),
        name="projections",
    )(device, w, s_high, s_low, modes, rim_inner, rim_outer, h)

    first_rows = leaf // 4

    def run_interpolate(start, size, token):
        return pl.pallas_call(
            functools.partial(interpolate, start=start),
            in_specs=[whole()] * 4,
            out_specs=whole(),
            out_shape=shape((size, rhs), BF16),
            compiler_params=params(4),
            cost_estimate=cost(4e9, 8e6),
            name="interpolate",
        )(s_high, s_low8, m, after(m8, token))

    def run_leaf(t0, t1, start, token):
        return pl.pallas_call(
            functools.partial(leaf_solve, start=start),
            in_specs=[whole()] * 4,
            out_specs=whole(),
            out_shape=shape((half_rows, rhs), F32),
            compiler_params=params(4),
            cost_estimate=cost(4.3e9, 10e6),
            name="leaf_solve",
        )(a_left, a_right, t0, after(t1, token))

    def run_stage(level, mine, other, before):
        if level == levels - 1:
            out_shape = [shape((ranks, half), F32)] * 2
            extra = before
        else:
            size = (mine.shape[0] - rank_k, half + h_width(level + 1))
            out_shape = [
                shape(size, F32),
                shape(size, BF16),
                shape((2 if level == 0 else 1, rank_k, half), F32),
            ]
            extra = []
        return pl.pallas_call(
            functools.partial(stage, level=level, levels=levels, rank_k=rank_k, half=half),
            in_specs=[scalars()] + [whole()] * (3 + len(extra)),
            out_specs=[whole()] * len(out_shape),
            out_shape=out_shape,
            compiler_params=params(6),
            cost_estimate=cost(1e8, 1e6),
            name="stage",
        )(device, cores, mine, other, *extra)

    parts = {}

    def beside(position, token):
        if position == 0:
            parts["t0"] = run_interpolate(0, first_rows, token)
            return parts["t0"]
        if position == 1:
            parts["t1"] = run_interpolate(first_rows, leaf - first_rows, token)
            return parts["t1"]
        if position == 2:
            parts["y0"] = run_leaf(parts["t0"], parts["t1"], 0, token)
            return parts["y0"]
        if position == 3:
            parts["y1"] = run_leaf(parts["t0"], parts["t1"], half_rows, token)
            return parts["y1"]
        return None

    before = []
    for level in range(levels):
        other = partner(send, level)
        token = beside(level, send)
        if token is not None:
            mine = after(mine, token)
        got = run_stage(level, mine, other, before)
        if level < levels - 1:
            mine, send = got[0], got[1]
            before.append(got[2])
    keep, send = got
    crossed = partner(send, 0)

    def run_update(c, before, own_half):
        return pl.pallas_call(
            functools.partial(update, own_half=own_half),
            in_specs=[scalars()] + [whole()] * 4 + [anywhere()] * len(before),
            out_specs=anywhere(),
            out_shape=pltpu.HBM((leaf, rhs), F32),
            input_output_aliases={5: 0} if before else {},
            scratch_shapes=[
                pltpu.VMEM((3 * ranks, half), BF16),
                pltpu.VMEM((leaf, half), F32),
                pltpu.SemaphoreType.DMA((leaf // 256,)),
            ],
            compiler_params=params(10),
            cost_estimate=cost(1.7e9, 9e6),
            name="update",
        )(device, left, parts["y0"], parts["y1"], c, *before)

    out = run_update(after(keep, send), [], True)
    return run_update(crossed, [out], False)


def solution(mesh):
    in_specs = (
        P(("groups", "narrow"), None),
        P(None, ("groups", "narrow")),
        P(None, ("groups", "narrow")),
        P(("groups", "narrow")),
        P(("groups", "narrow"), None),
        P(None, None, ("groups", "narrow")),
        P(None, None, ("groups", "narrow")),
        P("groups", None, None),
        P("groups"),
    )
    out_specs = P(("groups", "narrow"), None)
    return jax.shard_map(local, mesh=mesh, in_specs=in_specs, out_specs=out_specs, check_vma=False)
```

```python
import functools

import jax
import jax.numpy as jnp
from jax import lax
from jax.experimental import pallas as pl
from jax.experimental.pallas import tpu as pltpu
from jax.sharding import PartitionSpec as P

HALO = 128
LANES = 128
F32 = jnp.float32
BF16 = jnp.bfloat16
F8 = jnp.float8_e4m3fn
LOW_SCALE = 4096.0
NOWHERE_BITS = 11
NOWHERE = 2**NOWHERE_BITS - 1
MIB = 2**20


def whole():
    return pl.BlockSpec(memory_space=pltpu.VMEM)


def anywhere():
    return pl.BlockSpec(memory_space=pl.ANY)


def in_hbm(value):
    return pltpu.with_memory_space_constraint(value, pltpu.HBM)


def scalars():
    return pl.BlockSpec(memory_space=pltpu.SMEM)


def params(mib):
    return pltpu.CompilerParams(vmem_limit_bytes=mib * MIB)


def cost(flops, nbytes):
    return pl.CostEstimate(flops=int(flops), bytes_accessed=int(nbytes), transcendentals=0)


def ceil_to(value, unit):
    return -(-value // unit) * unit


def dot(a, b):
    return jnp.dot(a, b, preferred_element_type=F32)


def dot_split(a, b):
    a_high, a_low = split(a)
    b_high, b_low = split(b)
    return dot(a_high, b_high) + (dot(a_high, b_low) + dot(a_low, b_high))


def dot_nt(a, b):
    return lax.dot_general(a, b, (((1,), (1,)), ((), ())), preferred_element_type=F32)


def split(value):
    high = value.astype(BF16)
    return high, (value - high.astype(F32)).astype(BF16)


def masked_level(ref, rank_ref, level, rank_k):
    rows = ref[level * rank_k : (level + 1) * rank_k, :]
    place = lax.broadcasted_iota(jnp.int32, rows.shape, 0)
    return jnp.where(place < rank_ref[level], rows, 0.0)


def prepare(
    device_ref,
    rank_hbm,
    order_hbm,
    index_hbm,
    weight_hbm,
    modes_ref,
    core_ref,
    v_hbm,
    a_hbm,
    inner_ref,
    outer_ref,
    cols_ref,
    cores_ref,
    vs_ref,
    a_ref,
    rank_ref,
    order_ref,
    index_ref,
    weight_ref,
    v_ref,
    rows_scr,
    sems,
    *,
    levels,
    rank_k,
):
    own = modes_ref.shape[0]
    groups = order_ref.shape[0]
    device = device_ref[0]
    odd = jnp.bitwise_and(device, 1)
    inner = pl.multiple_of((1 - odd) * (own - HALO), HALO)
    outer = pl.multiple_of(odd * (own - HALO), HALO)
    cut = a_ref.shape[1]
    pairs = [
        (order_hbm, order_ref),
        (index_hbm, index_ref),
        (weight_hbm, weight_ref),
        (rank_hbm, rank_ref),
        (v_hbm, v_ref),
        (modes_ref.at[pl.ds(inner, HALO)], inner_ref),
        (modes_ref.at[pl.ds(outer, HALO)], outer_ref),
        (a_hbm.at[:, pl.ds(0, cut)], a_ref),
    ]
    for level in range(levels):
        slot = 2 ** (levels - 1 - level) - 1 + lax.shift_right_logical(device, level + 1)
        pairs.append((core_ref.at[slot], cores_ref.at[level]))
    copies = [
        pltpu.make_async_copy(source, target, sems.at[i])
        for i, (source, target) in enumerate(pairs)
    ]
    for copy in copies:
        copy.start()
    for copy in copies[:3]:
        copy.wait()

    rows_scr[...] = jnp.zeros(rows_scr.shape, F32)
    base = device * own
    for first in range(0, groups, 8):
        order = order_ref[first : first + 8, :]
        row_of = lax.shift_right_logical(order, 7)
        lane_of = jnp.bitwise_and(order, LANES - 1)
        taken = []
        for ref in (index_ref, weight_ref):
            for j in range(3):
                total = jnp.zeros((8, LANES), ref.dtype)
                for r in range(groups):
                    table = jnp.broadcast_to(ref[j : j + 1, r * LANES : (r + 1) * LANES], (8, LANES))
                    got = jnp.take_along_axis(table, lane_of, axis=1)
                    total = jnp.where(row_of == r, got, total)
                taken.append(total)
        cols = []
        for node in taken[:3]:
            node = node - base
            cols.append(
                jnp.where(
                    node < 0, node + (own + HALO), jnp.where(node >= own, node + HALO, node)
                )
            )
        w = taken[3:]
        for keep, drop in ((0, 2), (1, 2), (0, 1)):
            same = cols[drop] == cols[keep]
            w[keep] = w[keep] + jnp.where(same, w[drop], 0.0)
            cols[drop] = jnp.where(same, NOWHERE, cols[drop])
        packed = [cols[0] + cols[1] * (NOWHERE + 1), cols[2]]
        for quantity, value in enumerate([x.astype(F32) for x in packed] + w):
            for r in range(8):
                at = (first + r) * 8 + quantity
                rows_scr[at : at + 1, :] = value[r : r + 1, :]
    cols_ref[...] = rows_scr[...].T

    for copy in copies[3:5]:
        copy.wait()
    ranks = levels * rank_k
    for level in range(levels):
        high, low = split(masked_level(v_ref, rank_ref, level, rank_k))
        vs_ref[level * rank_k : (level + 1) * rank_k, :] = high
        vs_ref[ranks + level * rank_k : ranks + (level + 1) * rank_k, :] = low
    for copy in copies[5:]:
        copy.wait()


def leaf_operators(
    rank_hbm,
    cols_ref,
    v_split,
    u_hbm,
    a0_ref,
    a_hbm,
    sh_ref,
    sl_ref,
    s8_ref,
    w_ref,
    h_ref,
    left_ref,
    a1_ref,
    rank_ref,
    u_ref,
    sems,
    *,
    levels,
    rank_k,
):
    ranks = levels * rank_k
    leaf, width = sh_ref.shape
    piece = 256
    cut = a0_ref.shape[1]
    a_copies = {
        first: pltpu.make_async_copy(
            a_hbm.at[:, pl.ds(first, cut)], a1_ref.at[:, pl.ds(first - cut, cut)], sems.at[1 + first // cut]
        )
        for first in range(cut, leaf, cut)
    }
    rank_copy = pltpu.make_async_copy(rank_hbm, rank_ref, sems.at[0])
    u_copy = pltpu.make_async_copy(u_hbm, u_ref, sems.at[1])
    for copy in [rank_copy] + list(a_copies.values()) + [u_copy]:
        copy.start()

    lane = lax.broadcasted_iota(jnp.int32, (LANES, LANES), 1)
    zero = jnp.zeros((LANES, LANES), BF16)

    def build(group):
        def spread(j):
            at = group * 8 + j
            return jnp.broadcast_to(cols_ref[:, at : at + 1], (LANES, LANES))

        both = spread(0).astype(jnp.int32)
        index = [
            jnp.bitwise_and(both, NOWHERE),
            lax.shift_right_logical(both, NOWHERE_BITS),
            spread(1).astype(jnp.int32),
        ]
        index = [i.astype(jnp.int16) for i in index]
        high, low = [], []
        for j in range(3):
            weight = spread(2 + j)
            high.append(weight.astype(BF16))
            low.append(((weight - high[j].astype(F32)) * LOW_SCALE).astype(BF16))
        rows = slice(group * LANES, (group + 1) * LANES)
        for first in range(0, width, LANES):
            place = (lane + first).astype(jnp.int16)
            s_high, s_low = zero, zero
            for j in range(3):
                here = index[j] == place
                s_high = jnp.where(here, high[j], s_high)
                s_low = jnp.where(here, low[j], s_low)
            sh_ref[rows, first : first + LANES] = s_high
            sl_ref[rows, first : first + LANES] = s_low
            s8_ref[rows, first : first + LANES] = s_low.astype(F8)

    for at in range(0, leaf, piece):
        if at < cut:
            ref, first = a0_ref, at
        else:
            ref, first = a1_ref, at - cut
        if at in a_copies:
            a_copies[at].wait()
        block = slice(first, first + piece)
        w = dot(v_split[:ranks, :], ref[:, block])
        build(2 * (at // piece))
        w = w + dot(v_split[ranks:, :], ref[:, block])
        build(2 * (at // piece) + 1)
        high, low = split(w)
        w_ref[:ranks, at : at + piece] = high
        w_ref[ranks:, at : at + piece] = low
    rank_copy.wait()
    u_copy.wait()
    for level in range(levels):
        rows = slice(level * rank_k, (level + 1) * rank_k)
        u_ref[rows, :] = masked_level(u_ref, rank_ref, level, rank_k)
    high, low = split(u_ref[...])
    part = dot_nt(v_split[...], high)
    part = part[:ranks] + part[ranks:] + dot_nt(v_split[:ranks, :], low)
    for position, level in enumerate(range(levels - 2, -1, -1)):
        h_ref[:, position * rank_k : (position + 1) * rank_k] = part[
            :, level * rank_k : (level + 1) * rank_k
        ]
    used = (levels - 1) * rank_k
    if used < h_ref.shape[1]:
        h_ref[:, used:] = jnp.zeros((ranks, h_ref.shape[1] - used), F32)
    for first in range(0, u_ref.shape[1], piece):
        rows = slice(first, first + piece)
        high, low = split(u_ref[:, rows].T)
        left_ref[rows, :ranks] = high
        left_ref[rows, ranks:] = low


def projections(
    device_ref,
    w_ref,
    sh_ref,
    sl_ref,
    modes_ref,
    inner_ref,
    outer_ref,
    h_ref,
    keep_ref,
    send_ref,
    m_ref,
    m8_ref,
    ws_scr,
    p_scr,
):
    ranks = keep_ref.shape[0]
    own = modes_ref.shape[0]
    half = modes_ref.shape[1] // 2
    m_ref[:own, :] = modes_ref[...]
    core = jnp.bitwise_and(device_ref[0], 1)
    m_ref[pl.ds(pl.multiple_of(own + HALO - core * HALO, HALO), HALO), :] = inner_ref[...]
    m_ref[pl.ds(pl.multiple_of(own + core * HALO, HALO), HALO), :] = outer_ref[...]
    m8_ref[...] = m_ref[...].astype(F8)
    piece = 256
    for first in range(0, sh_ref.shape[1], piece):
        cols = slice(first, first + piece)
        part = dot(w_ref[...], sh_ref[:, cols])
        part = part[:ranks] + part[ranks:]
        part = part + dot(w_ref[:ranks, :], sl_ref[:, cols]) * (1.0 / LOW_SCALE)
        high, low = split(part)
        ws_scr[:ranks, cols] = high
        ws_scr[ranks:, cols] = low
    for first in range(0, 2 * half, piece):
        cols = slice(first, first + piece)
        part = dot(ws_scr[...], m_ref[:, cols])
        p_scr[:, cols] = part[:ranks] + part[ranks:]
    mine = pl.multiple_of(core * half, half)
    other = pl.multiple_of((1 - core) * half, half)
    keep_ref[:, :half] = p_scr[:, pl.ds(mine, half)]
    send_ref[:, :half] = p_scr[:, pl.ds(other, half)]
    keep_ref[:, half:] = h_ref[...]
    send_ref[:, half:] = h_ref[...]


def stage(device_ref, core_ref, mine_ref, other_ref, *refs, level, levels, rank_k, half):
    side = jnp.bitwise_and(lax.shift_right_logical(device_ref[0], level), 1)
    upper = jnp.full((rank_k, half), side, jnp.int32) == 1
    mine = mine_ref[:rank_k, :half]
    other = other_ref[:rank_k, :half].astype(F32)
    stack = jnp.concatenate([jnp.where(upper, other, mine), jnp.where(upper, mine, other)], axis=0)
    coef = dot_split(core_ref[level], stack)
    c_mine = jnp.where(upper, coef[:rank_k], coef[rank_k:])
    c_other = jnp.where(upper, coef[rank_k:], coef[:rank_k])
    if level < levels - 1:
        next_ref, send_ref, c_ref = refs[0], refs[1], refs[2]
        at = half + (levels - 2 - level) * rank_k
        h_mine = mine_ref[rank_k:, at : at + rank_k]
        h_other = other_ref[rank_k:, at : at + rank_k].astype(F32)
        q = mine_ref[rank_k:, :half] + other_ref[rank_k:, :half].astype(F32)
        q = q - dot_split(h_mine, c_mine) - dot_split(h_other, c_other)
        next_ref[:, :half] = q
        send_ref[:, :half] = q.astype(send_ref.dtype)
        end = next_ref.shape[1]
        if end > half:
            h = mine_ref[rank_k:, half:end] + other_ref[rank_k:, half:end].astype(F32)
            next_ref[:, half:] = h
            send_ref[:, half:] = h.astype(send_ref.dtype)
        c_ref[0] = c_mine
        if level == 0:
            c_ref[1] = c_other
    else:
        before, keep_ref, send_ref = refs[: levels - 1], refs[-2], refs[-1]
        for ref_level, ref in enumerate(before):
            rows = slice(ref_level * rank_k, (ref_level + 1) * rank_k)
            keep_ref[rows, :] = ref[0]
            send_ref[rows, :] = ref[1] if ref_level == 0 else ref[0]
        rows = slice(level * rank_k, (level + 1) * rank_k)
        keep_ref[rows, :] = c_mine
        send_ref[rows, :] = c_other if level == 0 else c_mine


def interpolate(sh_ref, s8_ref, m_ref, m8_ref, t_ref, *, start):
    block, piece = 512, 256
    for row in range(0, t_ref.shape[0], block):
        rows = slice(start + row, start + row + block)
        for first in range(0, t_ref.shape[1], piece):
            cols = slice(first, first + piece)
            part = dot(sh_ref[rows, :], m_ref[:, cols])
            part = part + dot(s8_ref[rows, :], m8_ref[:, cols]) * (1.0 / LOW_SCALE)
            t_ref[row : row + block, cols] = part.astype(BF16)


def leaf_solve(a0_ref, a1_ref, t0_ref, t1_ref, y_ref, *, start):
    block, piece = 512, 256
    for row in range(0, y_ref.shape[0], block):
        rows = slice(start + row, start + row + block)
        for first in range(0, y_ref.shape[1], piece):
            cols = slice(first, first + piece)
            part = dot(a0_ref[rows, :], t0_ref[:, cols]) + dot(a1_ref[rows, :], t1_ref[:, cols])
            y_ref[row : row + block, cols] = part


def update(device_ref, left_ref, y0_ref, y1_ref, c_ref, *refs, own_half):
    out_ref, c_scr, o_scr, sems = refs[-4:]
    ranks, half = c_ref.shape
    core = jnp.bitwise_and(device_ref[0], 1)
    at = pl.multiple_of((core if own_half else 1 - core) * half, half)
    high, low = split(c_ref[...])
    c_scr[:ranks, :] = high
    c_scr[ranks : 2 * ranks, :] = high
    c_scr[2 * ranks :, :] = low
    block, piece = 256, 256
    copies = []
    for row in range(0, o_scr.shape[0], block):
        rows = slice(row, row + block)
        if row < y0_ref.shape[0]:
            ref, begin = y0_ref, row
        else:
            ref, begin = y1_ref, row - y0_ref.shape[0]
        for first in range(0, half, piece):
            cols = slice(first, first + piece)
            part = dot(left_ref[rows, :], c_scr[: 2 * ranks, cols])
            part = part + dot(left_ref[rows, :ranks], c_scr[2 * ranks :, cols])
            solved = ref[begin : begin + block, pl.ds(pl.multiple_of(at + first, piece), piece)]
            o_scr[rows, cols] = solved - part
        copy = pltpu.make_async_copy(
            o_scr.at[pl.ds(row, block)],
            out_ref.at[pl.ds(row, block), pl.ds(at, half)],
            sems.at[row // block],
        )
        copy.start()
        copies.append(copy)
    for copy in copies:
        copy.wait()


def local(
    modes,
    node_index,
    interp_weight,
    leaf_order,
    leaf_inverse,
    v_factor,
    u_factor,
    core_table,
    level_rank,
):
    own, rhs = modes.shape
    half = rhs // 2
    levels, rank_k, leaf = v_factor.shape
    ranks = levels * rank_k
    count = lax.axis_size("narrow")
    device = lax.axis_index("narrow").astype(jnp.int32)
    device = device.reshape(1)
    width = own + 2 * HALO
    shape = pltpu.VMEM
    half_rows = leaf // 2
    first_rows = leaf // 4

    def partner(value, bit):
        return lax.ppermute(value, "narrow", [(s, s ^ (1 << bit)) for s in range(count)])

    def after(value, token):
        return lax.optimization_barrier((value, token))[0]

    v_rows = v_factor.reshape(ranks, leaf)
    u_rows = u_factor.reshape(ranks, leaf)

    def h_width(level):
        return ceil_to(rank_k * (levels - 1 - level), LANES)

    groups = leaf // LANES
    inner, outer, columns, cores, v_split, a_left = pl.pallas_call(
        functools.partial(prepare, levels=levels, rank_k=rank_k),
        in_specs=[scalars()] + [anywhere()] * 8,
        out_specs=[whole()] * 6,
        out_shape=[
            shape((HALO, rhs), BF16),
            shape((HALO, rhs), BF16),
            shape((LANES, groups * 8), F32),
            shape((levels, 2 * rank_k, 2 * rank_k), F32),
            shape((2 * ranks, leaf), BF16),
            shape((leaf, first_rows), BF16),
        ],
        scratch_shapes=[
            pltpu.SMEM((levels,), jnp.int32),
            pltpu.VMEM((groups, LANES), jnp.int32),
            pltpu.VMEM((3, leaf), jnp.int32),
            pltpu.VMEM((3, leaf), F32),
            pltpu.VMEM((ranks, leaf), F32),
            pltpu.VMEM((groups * 8, LANES), F32),
            pltpu.SemaphoreType.DMA((8 + levels,)),
        ],
        compiler_params=params(8),
        cost_estimate=cost(1e9, 8e6),
        name="prepare",
    )(
        device,
        in_hbm(level_rank),
        in_hbm(leaf_order.reshape(groups, LANES)),
        in_hbm(node_index),
        in_hbm(interp_weight),
        in_hbm(modes),
        in_hbm(core_table),
        in_hbm(v_rows),
        in_hbm(leaf_inverse),
    )

    rim_inner = partner(inner, 0)
    swaps = [(i, i + 1) for i in range(1, count - 1, 2)]
    rim_outer = lax.ppermute(outer, "narrow", swaps + [(j, i) for i, j in swaps])

    s_high, s_low, s_low8, w, h, left, a_right = pl.pallas_call(
        functools.partial(leaf_operators, levels=levels, rank_k=rank_k),
        in_specs=[anywhere(), whole(), whole(), anywhere(), whole(), anywhere()],
        out_specs=[whole()] * 7,
        out_shape=[
            shape((leaf, width), BF16),
            shape((leaf, width), BF16),
            shape((leaf, width), F8),
            shape((2 * ranks, leaf), BF16),
            shape((ranks, h_width(0)), F32),
            shape((leaf, 2 * ranks), BF16),
            shape((leaf, leaf - first_rows), BF16),
        ],
        scratch_shapes=[
            pltpu.SMEM((levels,), jnp.int32),
            pltpu.VMEM((ranks, leaf), F32),
            pltpu.SemaphoreType.DMA((1 + leaf // first_rows,)),
        ],
        compiler_params=params(12),
        cost_estimate=cost(5e9, 14e6),
        name="leaf_operators",
    )(in_hbm(level_rank), columns, v_split, in_hbm(u_rows), a_left, in_hbm(leaf_inverse))

    wide = half + h_width(0)
    mine, send, m, m8 = pl.pallas_call(
        projections,
        in_specs=[scalars()] + [whole()] * 7,
        out_specs=[whole()] * 4,
        out_shape=[
            shape((ranks, wide), F32),
            shape((ranks, wide), F32),
            shape((width, rhs), BF16),
            shape((width, rhs), F8),
        ],
        scratch_shapes=[pltpu.VMEM((2 * ranks, width), BF16), pltpu.VMEM((ranks, rhs), F32)],
        compiler_params=params(8),
        cost_estimate=cost(5e9, 14e6),
        name="projections",
    )(device, w, s_high, s_low, modes, rim_inner, rim_outer, h)

    def run_interpolate(start, size, token):
        return pl.pallas_call(
            functools.partial(interpolate, start=start),
            in_specs=[whole()] * 4,
            out_specs=whole(),
            out_shape=shape((size, rhs), BF16),
            compiler_params=params(4),
            cost_estimate=cost(4e9, 8e6),
            name="interpolate",
        )(s_high, s_low8, m, after(m8, token))

    def run_leaf(t0, t1, start, token):
        return pl.pallas_call(
            functools.partial(leaf_solve, start=start),
            in_specs=[whole()] * 4,
            out_specs=whole(),
            out_shape=shape((half_rows, rhs), F32),
            compiler_params=params(4),
            cost_estimate=cost(4.3e9, 10e6),
            name="leaf_solve",
        )(a_left, a_right, t0, after(t1, token))

    def run_stage(level, mine, other, before):
        if level == levels - 1:
            out_shape = [shape((ranks, half), F32)] * 2
            extra = before
        else:
            size = (mine.shape[0] - rank_k, half + h_width(level + 1))
            out_shape = [
                shape(size, F32),
                shape(size, BF16),
                shape((2 if level == 0 else 1, rank_k, half), F32),
            ]
            extra = []
        return pl.pallas_call(
            functools.partial(stage, level=level, levels=levels, rank_k=rank_k, half=half),
            in_specs=[scalars()] + [whole()] * (3 + len(extra)),
            out_specs=[whole()] * len(out_shape),
            out_shape=out_shape,
            compiler_params=params(6),
            cost_estimate=cost(1e8, 1e6),
            name="stage",
        )(device, cores, mine, other, *extra)

    parts = {}

    def beside(position, token):
        if position == 0:
            parts["t0"] = run_interpolate(0, first_rows, token)
            return parts["t0"]
        if position == 1:
            parts["t1"] = run_interpolate(first_rows, leaf - first_rows, token)
            return parts["t1"]
        if position == 2:
            parts["y0"] = run_leaf(parts["t0"], parts["t1"], 0, token)
            return parts["y0"]
        if position == 3:
            parts["y1"] = run_leaf(parts["t0"], parts["t1"], half_rows, token)
            return parts["y1"]
        return None

    before = []
    for level in range(levels):
        other = partner(send, level)
        token = beside(level, send)
        if token is not None:
            mine = after(mine, token)
        got = run_stage(level, mine, other, before)
        if level < levels - 1:
            mine, send = got[0], got[1]
            before.append(got[2])
    keep, send = got
    crossed = partner(send, 0)

    def run_update(c, before, own_half):
        return pl.pallas_call(
            functools.partial(update, own_half=own_half),
            in_specs=[scalars()] + [whole()] * 4 + [anywhere()] * len(before),
            out_specs=anywhere(),
            out_shape=pltpu.HBM((leaf, rhs), F32),
            input_output_aliases={5: 0} if before else {},
            scratch_shapes=[
                pltpu.VMEM((3 * ranks, half), BF16),
                pltpu.VMEM((leaf, half), F32),
                pltpu.SemaphoreType.DMA((leaf // 256,)),
            ],
            compiler_params=params(10),
            cost_estimate=cost(1.7e9, 9e6),
            name="update",
        )(device, left, parts["y0"], parts["y1"], c, *before)

    out = run_update(after(keep, send), [], True)
    return run_update(crossed, [out], False)


def solution(mesh):
    in_specs = (
        P(("groups", "narrow"), None),
        P(None, ("groups", "narrow")),
        P(None, ("groups", "narrow")),
        P(("groups", "narrow")),
        P(("groups", "narrow"), None),
        P(None, None, ("groups", "narrow")),
        P(None, None, ("groups", "narrow")),
        P("groups", None, None),
        P("groups"),
    )
    out_specs = P(("groups", "narrow"), None)
    return jax.shard_map(local, mesh=mesh, in_specs=in_specs, out_specs=out_specs, check_vma=False)
```

```python
import functools

import jax
import jax.numpy as jnp
from jax import lax
from jax.experimental import pallas as pl
from jax.experimental.pallas import tpu as pltpu
from jax.sharding import PartitionSpec as P

HALO = 128
LANES = 128
F32 = jnp.float32
BF16 = jnp.bfloat16
F8 = jnp.float8_e4m3fn
LOW_SCALE = 4096.0
W8_TOP = 224.0
TINY = 1e-30
NOWHERE_BITS = 11
NOWHERE = 2**NOWHERE_BITS - 1
MIB = 2**20


def whole():
    return pl.BlockSpec(memory_space=pltpu.VMEM)


def anywhere():
    return pl.BlockSpec(memory_space=pl.ANY)


def in_hbm(value):
    return pltpu.with_memory_space_constraint(value, pltpu.HBM)


def scalars():
    return pl.BlockSpec(memory_space=pltpu.SMEM)


def params(mib):
    return pltpu.CompilerParams(vmem_limit_bytes=mib * MIB)


def cost(flops, nbytes):
    return pl.CostEstimate(flops=int(flops), bytes_accessed=int(nbytes), transcendentals=0)


def ceil_to(value, unit):
    return -(-value // unit) * unit


def dot(a, b):
    return jnp.dot(a, b, preferred_element_type=F32)


def dot_split(a, b):
    a_high, a_low = split(a)
    b_high, b_low = split(b)
    return dot(a_high, b_high) + (dot(a_high, b_low) + dot(a_low, b_high))


def dot_nt(a, b):
    return lax.dot_general(a, b, (((1,), (1,)), ((), ())), preferred_element_type=F32)


def split(value):
    high = value.astype(BF16)
    return high, (value - high.astype(F32)).astype(BF16)


def masked_level(ref, rank_ref, level, rank_k):
    rows = ref[level * rank_k : (level + 1) * rank_k, :]
    place = lax.broadcasted_iota(jnp.int32, rows.shape, 0)
    return jnp.where(place < rank_ref[level], rows, 0.0)


def prepare(
    device_ref,
    rank_hbm,
    order_hbm,
    index_hbm,
    weight_hbm,
    modes_ref,
    core_ref,
    v_hbm,
    a_hbm,
    inner_ref,
    outer_ref,
    cols_ref,
    cores_ref,
    vs_ref,
    a_ref,
    rank_ref,
    order_ref,
    index_ref,
    weight_ref,
    v_ref,
    rows_scr,
    sems,
    *,
    levels,
    rank_k,
):
    own = modes_ref.shape[0]
    groups = order_ref.shape[0]
    device = device_ref[0]
    odd = jnp.bitwise_and(device, 1)
    inner = pl.multiple_of((1 - odd) * (own - HALO), HALO)
    outer = pl.multiple_of(odd * (own - HALO), HALO)
    cut = a_ref.shape[1]
    pairs = [
        (order_hbm, order_ref),
        (index_hbm, index_ref),
        (weight_hbm, weight_ref),
        (rank_hbm, rank_ref),
        (v_hbm, v_ref),
        (modes_ref.at[pl.ds(inner, HALO)], inner_ref),
        (modes_ref.at[pl.ds(outer, HALO)], outer_ref),
        (a_hbm.at[:, pl.ds(0, cut)], a_ref),
    ]
    for level in range(levels):
        slot = 2 ** (levels - 1 - level) - 1 + lax.shift_right_logical(device, level + 1)
        pairs.append((core_ref.at[slot], cores_ref.at[level]))
    copies = [
        pltpu.make_async_copy(source, target, sems.at[i])
        for i, (source, target) in enumerate(pairs)
    ]
    for copy in copies:
        copy.start()
    for copy in copies[:3]:
        copy.wait()

    rows_scr[...] = jnp.zeros(rows_scr.shape, F32)
    base = device * own
    for first in range(0, groups, 8):
        order = order_ref[first : first + 8, :]
        row_of = lax.shift_right_logical(order, 7)
        lane_of = jnp.bitwise_and(order, LANES - 1)
        taken = []
        for ref in (index_ref, weight_ref):
            for j in range(3):
                total = jnp.zeros((8, LANES), ref.dtype)
                for r in range(groups):
                    table = jnp.broadcast_to(ref[j : j + 1, r * LANES : (r + 1) * LANES], (8, LANES))
                    got = jnp.take_along_axis(table, lane_of, axis=1)
                    total = jnp.where(row_of == r, got, total)
                taken.append(total)
        cols = []
        for node in taken[:3]:
            node = node - base
            cols.append(
                jnp.where(
                    node < 0, node + (own + HALO), jnp.where(node >= own, node + HALO, node)
                )
            )
        w = taken[3:]
        for keep, drop in ((0, 2), (1, 2), (0, 1)):
            same = cols[drop] == cols[keep]
            w[keep] = w[keep] + jnp.where(same, w[drop], 0.0)
            cols[drop] = jnp.where(same, NOWHERE, cols[drop])
        packed = [cols[0] + cols[1] * (NOWHERE + 1), cols[2]]
        for quantity, value in enumerate([x.astype(F32) for x in packed] + w):
            for r in range(8):
                at = (first + r) * 8 + quantity
                rows_scr[at : at + 1, :] = value[r : r + 1, :]
    cols_ref[...] = rows_scr[...].T

    for copy in copies[3:5]:
        copy.wait()
    ranks = levels * rank_k
    for level in range(levels):
        high, low = split(masked_level(v_ref, rank_ref, level, rank_k))
        vs_ref[level * rank_k : (level + 1) * rank_k, :] = high
        vs_ref[ranks + level * rank_k : ranks + (level + 1) * rank_k, :] = low
    for copy in copies[5:]:
        copy.wait()


def leaf_operators(
    rank_hbm,
    cols_ref,
    v_split,
    u_hbm,
    a0_ref,
    a_hbm,
    sh_ref,
    s8_ref,
    w_ref,
    h_ref,
    left_ref,
    a1_ref,
    rank_ref,
    u_ref,
    sems,
    *,
    levels,
    rank_k,
):
    ranks = levels * rank_k
    leaf, width = sh_ref.shape
    piece = 256
    cut = a0_ref.shape[1]
    a_copies = {
        first: pltpu.make_async_copy(
            a_hbm.at[:, pl.ds(first, cut)], a1_ref.at[:, pl.ds(first - cut, cut)], sems.at[1 + first // cut]
        )
        for first in range(cut, leaf, cut)
    }
    rank_copy = pltpu.make_async_copy(rank_hbm, rank_ref, sems.at[0])
    u_copy = pltpu.make_async_copy(u_hbm, u_ref, sems.at[1])
    for copy in [rank_copy] + list(a_copies.values()) + [u_copy]:
        copy.start()

    lane = lax.broadcasted_iota(jnp.int32, (LANES, LANES), 1)
    zero = jnp.zeros((LANES, LANES), BF16)

    def build(group):
        def spread(j):
            at = group * 8 + j
            return jnp.broadcast_to(cols_ref[:, at : at + 1], (LANES, LANES))

        both = spread(0).astype(jnp.int32)
        index = [
            jnp.bitwise_and(both, NOWHERE),
            lax.shift_right_logical(both, NOWHERE_BITS),
            spread(1).astype(jnp.int32),
        ]
        index = [i.astype(jnp.int16) for i in index]
        high, low = [], []
        for j in range(3):
            weight = spread(2 + j)
            high.append(weight.astype(BF16))
            low.append(((weight - high[j].astype(F32)) * LOW_SCALE).astype(BF16))
        rows = slice(group * LANES, (group + 1) * LANES)
        for first in range(0, width, LANES):
            place = (lane + first).astype(jnp.int16)
            s_high, s_low = zero, zero
            for j in range(3):
                here = index[j] == place
                s_high = jnp.where(here, high[j], s_high)
                s_low = jnp.where(here, low[j], s_low)
            sh_ref[rows, first : first + LANES] = s_high
            s8_ref[rows, first : first + LANES] = s_low.astype(F8)

    for at in range(0, leaf, piece):
        if at < cut:
            ref, first = a0_ref, at
        else:
            ref, first = a1_ref, at - cut
        if at in a_copies:
            a_copies[at].wait()
        block = slice(first, first + piece)
        w = dot(v_split[:ranks, :], ref[:, block])
        build(2 * (at // piece))
        w = w + dot(v_split[ranks:, :], ref[:, block])
        build(2 * (at // piece) + 1)
        high, low = split(w)
        w_ref[:ranks, at : at + piece] = high
        w_ref[ranks:, at : at + piece] = low
    rank_copy.wait()
    u_copy.wait()
    for level in range(levels):
        rows = slice(level * rank_k, (level + 1) * rank_k)
        u_ref[rows, :] = masked_level(u_ref, rank_ref, level, rank_k)
    high, low = split(u_ref[...])
    part = dot_nt(v_split[...], high)
    part = part[:ranks] + part[ranks:] + dot_nt(v_split[:ranks, :], low)
    for position, level in enumerate(range(levels - 2, -1, -1)):
        h_ref[:, position * rank_k : (position + 1) * rank_k] = part[
            :, level * rank_k : (level + 1) * rank_k
        ]
    used = (levels - 1) * rank_k
    if used < h_ref.shape[1]:
        h_ref[:, used:] = jnp.zeros((ranks, h_ref.shape[1] - used), F32)
    for first in range(0, u_ref.shape[1], piece):
        rows = slice(first, first + piece)
        high, low = split(u_ref[:, rows].T)
        left_ref[rows, :ranks] = high
        left_ref[rows, ranks:] = low


def projections(
    device_ref,
    w_ref,
    sh_ref,
    s8_ref,
    modes_ref,
    inner_ref,
    outer_ref,
    h_ref,
    keep_ref,
    send_ref,
    m_ref,
    m8_ref,
    w8_scr,
    ws_scr,
    p_scr,
):
    ranks = keep_ref.shape[0]
    own = modes_ref.shape[0]
    half = modes_ref.shape[1] // 2
    m_ref[:own, :] = modes_ref[...]
    core = jnp.bitwise_and(device_ref[0], 1)
    m_ref[pl.ds(pl.multiple_of(own + HALO - core * HALO, HALO), HALO), :] = inner_ref[...]
    m_ref[pl.ds(pl.multiple_of(own + core * HALO, HALO), HALO), :] = outer_ref[...]
    m8_ref[...] = m_ref[...].astype(F8)
    piece = 256
    pieces = [slice(first, first + piece) for first in range(0, sh_ref.shape[1], piece)]

    def main_part(cols):
        part = dot(w_ref[...], sh_ref[:, cols])
        return part[:ranks] + part[ranks:]

    parts = [main_part(pieces[0])]
    largest = jnp.max(jnp.abs(w_ref[:ranks, :].astype(F32)), axis=1, keepdims=True)
    largest = jnp.maximum(largest, TINY)
    parts.append(main_part(pieces[1]))
    w8_scr[...] = (w_ref[:ranks, :].astype(F32) * (W8_TOP / largest)).astype(F8)
    w_back = largest * (1.0 / (W8_TOP * LOW_SCALE))
    for i, cols in enumerate(pieces):
        if i + 2 < len(pieces):
            parts.append(main_part(pieces[i + 2]))
        part = parts[i] + dot(w8_scr[...], s8_ref[:, cols]) * w_back
        high, low = split(part)
        ws_scr[:ranks, cols] = high
        ws_scr[ranks:, cols] = low
    for first in range(0, 2 * half, piece):
        cols = slice(first, first + piece)
        part = dot(ws_scr[...], m_ref[:, cols])
        p_scr[:, cols] = part[:ranks] + part[ranks:]
    mine = pl.multiple_of(core * half, half)
    other = pl.multiple_of((1 - core) * half, half)
    keep_ref[:, :half] = p_scr[:, pl.ds(mine, half)]
    send_ref[:, :half] = p_scr[:, pl.ds(other, half)]
    keep_ref[:, half:] = h_ref[...]
    send_ref[:, half:] = h_ref[...]


def stage(device_ref, core_ref, mine_ref, other_ref, *refs, level, levels, rank_k, half):
    side = jnp.bitwise_and(lax.shift_right_logical(device_ref[0], level), 1)
    upper = jnp.full((rank_k, half), side, jnp.int32) == 1
    mine = mine_ref[:rank_k, :half]
    other = other_ref[:rank_k, :half].astype(F32)
    stack = jnp.concatenate([jnp.where(upper, other, mine), jnp.where(upper, mine, other)], axis=0)
    coef = dot_split(core_ref[level], stack)
    c_mine = jnp.where(upper, coef[:rank_k], coef[rank_k:])
    c_other = jnp.where(upper, coef[rank_k:], coef[:rank_k])
    if level < levels - 1:
        next_ref, send_ref, c_ref = refs[0], refs[1], refs[2]
        at = half + (levels - 2 - level) * rank_k
        h_mine = mine_ref[rank_k:, at : at + rank_k]
        h_other = other_ref[rank_k:, at : at + rank_k].astype(F32)
        q = mine_ref[rank_k:, :half] + other_ref[rank_k:, :half].astype(F32)
        q = q - dot_split(h_mine, c_mine) - dot_split(h_other, c_other)
        next_ref[:, :half] = q
        send_ref[:, :half] = q.astype(send_ref.dtype)
        end = next_ref.shape[1]
        if end > half:
            h = mine_ref[rank_k:, half:end] + other_ref[rank_k:, half:end].astype(F32)
            next_ref[:, half:] = h
            send_ref[:, half:] = h.astype(send_ref.dtype)
        c_ref[0] = c_mine
        if level == 0:
            c_ref[1] = c_other
    else:
        before, keep_ref, send_ref = refs[: levels - 1], refs[-2], refs[-1]
        for ref_level, ref in enumerate(before):
            rows = slice(ref_level * rank_k, (ref_level + 1) * rank_k)
            keep_ref[rows, :] = ref[0]
            send_ref[rows, :] = ref[1] if ref_level == 0 else ref[0]
        rows = slice(level * rank_k, (level + 1) * rank_k)
        keep_ref[rows, :] = c_mine
        send_ref[rows, :] = c_other if level == 0 else c_mine


def interpolate(sh_ref, s8_ref, m_ref, m8_ref, t_ref, *, start):
    block, piece = 512, 256
    for row in range(0, t_ref.shape[0], block):
        rows = slice(start + row, start + row + block)
        for first in range(0, t_ref.shape[1], piece):
            cols = slice(first, first + piece)
            part = dot(sh_ref[rows, :], m_ref[:, cols])
            part = part + dot(s8_ref[rows, :], m8_ref[:, cols]) * (1.0 / LOW_SCALE)
            t_ref[row : row + block, cols] = part.astype(BF16)


def leaf_solve(a0_ref, a1_ref, t0_ref, t1_ref, y_ref, *, start):
    block, piece = 512, 256
    for row in range(0, y_ref.shape[0], block):
        rows = slice(start + row, start + row + block)
        for first in range(0, y_ref.shape[1], piece):
            cols = slice(first, first + piece)
            part = dot(a0_ref[rows, :], t0_ref[:, cols]) + dot(a1_ref[rows, :], t1_ref[:, cols])
            y_ref[row : row + block, cols] = part


def update(device_ref, left_ref, y0_ref, y1_ref, c_ref, *refs, own_half):
    out_ref, c_scr, o_scr, sems = refs[-4:]
    ranks, half = c_ref.shape
    core = jnp.bitwise_and(device_ref[0], 1)
    at = pl.multiple_of((core if own_half else 1 - core) * half, half)
    high, low = split(c_ref[...])
    c_scr[:ranks, :] = high
    c_scr[ranks : 2 * ranks, :] = high
    c_scr[2 * ranks :, :] = low
    block, piece = 256, 256
    copies = []
    for row in range(0, o_scr.shape[0], block):
        rows = slice(row, row + block)
        if row < y0_ref.shape[0]:
            ref, begin = y0_ref, row
        else:
            ref, begin = y1_ref, row - y0_ref.shape[0]
        for first in range(0, half, piece):
            cols = slice(first, first + piece)
            part = dot(left_ref[rows, :], c_scr[: 2 * ranks, cols])
            part = part + dot(left_ref[rows, :ranks], c_scr[2 * ranks :, cols])
            solved = ref[begin : begin + block, pl.ds(pl.multiple_of(at + first, piece), piece)]
            o_scr[rows, cols] = solved - part
        copy = pltpu.make_async_copy(
            o_scr.at[pl.ds(row, block)],
            out_ref.at[pl.ds(row, block), pl.ds(at, half)],
            sems.at[row // block],
        )
        copy.start()
        copies.append(copy)
    for copy in copies:
        copy.wait()


def local(
    modes,
    node_index,
    interp_weight,
    leaf_order,
    leaf_inverse,
    v_factor,
    u_factor,
    core_table,
    level_rank,
):
    own, rhs = modes.shape
    half = rhs // 2
    levels, rank_k, leaf = v_factor.shape
    ranks = levels * rank_k
    count = lax.axis_size("narrow")
    device = lax.axis_index("narrow").astype(jnp.int32)
    device = device.reshape(1)
    width = own + 2 * HALO
    shape = pltpu.VMEM
    half_rows = leaf // 2
    first_rows = leaf // 4

    def partner(value, bit):
        return lax.ppermute(value, "narrow", [(s, s ^ (1 << bit)) for s in range(count)])

    def after(value, token):
        return lax.optimization_barrier((value, token))[0]

    v_rows = v_factor.reshape(ranks, leaf)
    u_rows = u_factor.reshape(ranks, leaf)

    def h_width(level):
        return ceil_to(rank_k * (levels - 1 - level), LANES)

    groups = leaf // LANES
    inner, outer, columns, cores, v_split, a_left = pl.pallas_call(
        functools.partial(prepare, levels=levels, rank_k=rank_k),
        in_specs=[scalars()] + [anywhere()] * 8,
        out_specs=[whole()] * 6,
        out_shape=[
            shape((HALO, rhs), BF16),
            shape((HALO, rhs), BF16),
            shape((LANES, groups * 8), F32),
            shape((levels, 2 * rank_k, 2 * rank_k), F32),
            shape((2 * ranks, leaf), BF16),
            shape((leaf, first_rows), BF16),
        ],
        scratch_shapes=[
            pltpu.SMEM((levels,), jnp.int32),
            pltpu.VMEM((groups, LANES), jnp.int32),
            pltpu.VMEM((3, leaf), jnp.int32),
            pltpu.VMEM((3, leaf), F32),
            pltpu.VMEM((ranks, leaf), F32),
            pltpu.VMEM((groups * 8, LANES), F32),
            pltpu.SemaphoreType.DMA((8 + levels,)),
        ],
        compiler_params=params(8),
        cost_estimate=cost(1e9, 8e6),
        name="prepare",
    )(
        device,
        in_hbm(level_rank),
        in_hbm(leaf_order.reshape(groups, LANES)),
        in_hbm(node_index),
        in_hbm(interp_weight),
        in_hbm(modes),
        in_hbm(core_table),
        in_hbm(v_rows),
        in_hbm(leaf_inverse),
    )

    rim_inner = partner(inner, 0)
    swaps = [(i, i + 1) for i in range(1, count - 1, 2)]
    rim_outer = lax.ppermute(outer, "narrow", swaps + [(j, i) for i, j in swaps])

    s_high, s_low8, w, h, left, a_right = pl.pallas_call(
        functools.partial(leaf_operators, levels=levels, rank_k=rank_k),
        in_specs=[anywhere(), whole(), whole(), anywhere(), whole(), anywhere()],
        out_specs=[whole()] * 6,
        out_shape=[
            shape((leaf, width), BF16),
            shape((leaf, width), F8),
            shape((2 * ranks, leaf), BF16),
            shape((ranks, h_width(0)), F32),
            shape((leaf, 2 * ranks), BF16),
            shape((leaf, leaf - first_rows), BF16),
        ],
        scratch_shapes=[
            pltpu.SMEM((levels,), jnp.int32),
            pltpu.VMEM((ranks, leaf), F32),
            pltpu.SemaphoreType.DMA((1 + leaf // first_rows,)),
        ],
        compiler_params=params(12),
        cost_estimate=cost(5e9, 14e6),
        name="leaf_operators",
    )(in_hbm(level_rank), columns, v_split, in_hbm(u_rows), a_left, in_hbm(leaf_inverse))

    wide = half + h_width(0)
    mine, send, m, m8 = pl.pallas_call(
        projections,
        in_specs=[scalars()] + [whole()] * 7,
        out_specs=[whole()] * 4,
        out_shape=[
            shape((ranks, wide), F32),
            shape((ranks, wide), F32),
            shape((width, rhs), BF16),
            shape((width, rhs), F8),
        ],
        scratch_shapes=[
            pltpu.VMEM((ranks, leaf), F8),
            pltpu.VMEM((2 * ranks, width), BF16),
            pltpu.VMEM((ranks, rhs), F32),
        ],
        compiler_params=params(8),
        cost_estimate=cost(5e9, 14e6),
        name="projections",
    )(device, w, s_high, s_low8, modes, rim_inner, rim_outer, h)

    def run_interpolate(start, size, token):
        return pl.pallas_call(
            functools.partial(interpolate, start=start),
            in_specs=[whole()] * 4,
            out_specs=whole(),
            out_shape=shape((size, rhs), BF16),
            compiler_params=params(4),
            cost_estimate=cost(4e9, 8e6),
            name="interpolate",
        )(s_high, s_low8, m, after(m8, token))

    def run_leaf(t0, t1, start, token):
        return pl.pallas_call(
            functools.partial(leaf_solve, start=start),
            in_specs=[whole()] * 4,
            out_specs=whole(),
            out_shape=shape((half_rows, rhs), F32),
            compiler_params=params(4),
            cost_estimate=cost(4.3e9, 10e6),
            name="leaf_solve",
        )(a_left, a_right, t0, after(t1, token))

    def run_stage(level, mine, other, before):
        if level == levels - 1:
            out_shape = [shape((ranks, half), F32)] * 2
            extra = before
        else:
            size = (mine.shape[0] - rank_k, half + h_width(level + 1))
            out_shape = [
                shape(size, F32),
                shape(size, BF16),
                shape((2 if level == 0 else 1, rank_k, half), F32),
            ]
            extra = []
        return pl.pallas_call(
            functools.partial(stage, level=level, levels=levels, rank_k=rank_k, half=half),
            in_specs=[scalars()] + [whole()] * (3 + len(extra)),
            out_specs=[whole()] * len(out_shape),
            out_shape=out_shape,
            compiler_params=params(6),
            cost_estimate=cost(1e8, 1e6),
            name="stage",
        )(device, cores, mine, other, *extra)

    parts = {}

    def beside(position, token):
        if position == 0:
            parts["t0"] = run_interpolate(0, first_rows, token)
            return parts["t0"]
        if position == 1:
            parts["t1"] = run_interpolate(first_rows, leaf - first_rows, token)
            return parts["t1"]
        if position == 2:
            parts["y0"] = run_leaf(parts["t0"], parts["t1"], 0, token)
            return parts["y0"]
        if position == 3:
            parts["y1"] = run_leaf(parts["t0"], parts["t1"], half_rows, token)
            return parts["y1"]
        return None

    before = []
    for level in range(levels):
        other = partner(send, level)
        token = beside(level, send)
        if token is not None:
            mine = after(mine, token)
        got = run_stage(level, mine, other, before)
        if level < levels - 1:
            mine, send = got[0], got[1]
            before.append(got[2])
    keep, send = got
    crossed = partner(send, 0)

    def run_update(c, before, own_half):
        return pl.pallas_call(
            functools.partial(update, own_half=own_half),
            in_specs=[scalars()] + [whole()] * 4 + [anywhere()] * len(before),
            out_specs=anywhere(),
            out_shape=pltpu.HBM((leaf, rhs), F32),
            input_output_aliases={5: 0} if before else {},
            scratch_shapes=[
                pltpu.VMEM((3 * ranks, half), BF16),
                pltpu.VMEM((leaf, half), F32),
                pltpu.SemaphoreType.DMA((leaf // 256,)),
            ],
            compiler_params=params(10),
            cost_estimate=cost(1.7e9, 9e6),
            name="update",
        )(device, left, parts["y0"], parts["y1"], c, *before)

    out = run_update(after(keep, send), [], True)
    return run_update(crossed, [out], False)


def solution(mesh):
    in_specs = (
        P(("groups", "narrow"), None),
        P(None, ("groups", "narrow")),
        P(None, ("groups", "narrow")),
        P(("groups", "narrow")),
        P(("groups", "narrow"), None),
        P(None, None, ("groups", "narrow")),
        P(None, None, ("groups", "narrow")),
        P("groups", None, None),
        P("groups"),
    )
    out_specs = P(("groups", "narrow"), None)
    return jax.shard_map(local, mesh=mesh, in_specs=in_specs, out_specs=out_specs, check_vma=False)
```

```python
import functools

import jax
import jax.numpy as jnp
from jax import lax
from jax.experimental import pallas as pl
from jax.experimental.pallas import tpu as pltpu
from jax.sharding import PartitionSpec as P

HALO = 128
LANES = 128
F32 = jnp.float32
BF16 = jnp.bfloat16
F8 = jnp.float8_e4m3fn
LOW_SCALE = 4096.0
W8_TOP = 224.0
W_LOW = 256.0
TINY = 1e-30
NOWHERE_BITS = 11
NOWHERE = 2**NOWHERE_BITS - 1
MIB = 2**20


def whole():
    return pl.BlockSpec(memory_space=pltpu.VMEM)


def anywhere():
    return pl.BlockSpec(memory_space=pl.ANY)


def in_hbm(value):
    return pltpu.with_memory_space_constraint(value, pltpu.HBM)


def scalars():
    return pl.BlockSpec(memory_space=pltpu.SMEM)


def params(mib):
    return pltpu.CompilerParams(vmem_limit_bytes=mib * MIB)


def cost(flops, nbytes):
    return pl.CostEstimate(flops=int(flops), bytes_accessed=int(nbytes), transcendentals=0)


def ceil_to(value, unit):
    return -(-value // unit) * unit


def dot(a, b):
    return jnp.dot(a, b, preferred_element_type=F32)


def dot_split(a, b):
    a_high, a_low = split(a)
    b_high, b_low = split(b)
    return dot(a_high, b_high) + (dot(a_high, b_low) + dot(a_low, b_high))


def dot_nt(a, b):
    return lax.dot_general(a, b, (((1,), (1,)), ((), ())), preferred_element_type=F32)


def split(value):
    high = value.astype(BF16)
    return high, (value - high.astype(F32)).astype(BF16)


def masked_level(ref, rank_ref, level, rank_k):
    rows = ref[level * rank_k : (level + 1) * rank_k, :]
    place = lax.broadcasted_iota(jnp.int32, rows.shape, 0)
    return jnp.where(place < rank_ref[level], rows, 0.0)


def prepare(
    device_ref,
    rank_hbm,
    order_hbm,
    index_hbm,
    weight_hbm,
    modes_ref,
    core_ref,
    v_hbm,
    a_hbm,
    inner_ref,
    outer_ref,
    cols_ref,
    cores_ref,
    vs_ref,
    a_ref,
    rank_ref,
    order_ref,
    index_ref,
    weight_ref,
    v_ref,
    rows_scr,
    sems,
    *,
    levels,
    rank_k,
):
    own = modes_ref.shape[0]
    groups = order_ref.shape[0]
    device = device_ref[0]
    odd = jnp.bitwise_and(device, 1)
    inner = pl.multiple_of((1 - odd) * (own - HALO), HALO)
    outer = pl.multiple_of(odd * (own - HALO), HALO)
    cut = a_ref.shape[1]
    pairs = [
        (order_hbm, order_ref),
        (index_hbm, index_ref),
        (weight_hbm, weight_ref),
        (rank_hbm, rank_ref),
        (v_hbm, v_ref),
        (modes_ref.at[pl.ds(inner, HALO)], inner_ref),
        (modes_ref.at[pl.ds(outer, HALO)], outer_ref),
        (a_hbm.at[:, pl.ds(0, cut)], a_ref),
    ]
    for level in range(levels):
        slot = 2 ** (levels - 1 - level) - 1 + lax.shift_right_logical(device, level + 1)
        pairs.append((core_ref.at[slot], cores_ref.at[level]))
    copies = [
        pltpu.make_async_copy(source, target, sems.at[i])
        for i, (source, target) in enumerate(pairs)
    ]
    for copy in copies:
        copy.start()
    for copy in copies[:3]:
        copy.wait()

    rows_scr[...] = jnp.zeros(rows_scr.shape, F32)
    base = device * own
    for first in range(0, groups, 8):
        order = order_ref[first : first + 8, :]
        row_of = lax.shift_right_logical(order, 7)
        lane_of = jnp.bitwise_and(order, LANES - 1)
        taken = []
        for ref in (index_ref, weight_ref):
            for j in range(3):
                total = jnp.zeros((8, LANES), ref.dtype)
                for r in range(groups):
                    table = jnp.broadcast_to(ref[j : j + 1, r * LANES : (r + 1) * LANES], (8, LANES))
                    got = jnp.take_along_axis(table, lane_of, axis=1)
                    total = jnp.where(row_of == r, got, total)
                taken.append(total)
        cols = []
        for node in taken[:3]:
            node = node - base
            cols.append(
                jnp.where(
                    node < 0, node + (own + HALO), jnp.where(node >= own, node + HALO, node)
                )
            )
        w = taken[3:]
        for keep, drop in ((0, 2), (1, 2), (0, 1)):
            same = cols[drop] == cols[keep]
            w[keep] = w[keep] + jnp.where(same, w[drop], 0.0)
            cols[drop] = jnp.where(same, NOWHERE, cols[drop])
        packed = [cols[0] + cols[1] * (NOWHERE + 1), cols[2]]
        for quantity, value in enumerate([x.astype(F32) for x in packed] + w):
            for r in range(8):
                at = (first + r) * 8 + quantity
                rows_scr[at : at + 1, :] = value[r : r + 1, :]
    cols_ref[...] = rows_scr[...].T

    for copy in copies[3:5]:
        copy.wait()
    ranks = levels * rank_k
    for level in range(levels):
        high, low = split(masked_level(v_ref, rank_ref, level, rank_k))
        vs_ref[level * rank_k : (level + 1) * rank_k, :] = high
        vs_ref[ranks + level * rank_k : ranks + (level + 1) * rank_k, :] = low
    for copy in copies[5:]:
        copy.wait()


def leaf_operators(
    rank_hbm,
    cols_ref,
    v_split,
    u_hbm,
    a0_ref,
    a_hbm,
    sh_ref,
    s8_ref,
    w_ref,
    h_ref,
    left_ref,
    a1_ref,
    rank_ref,
    u_ref,
    sems,
    *,
    levels,
    rank_k,
):
    ranks = levels * rank_k
    leaf, width = sh_ref.shape
    piece = 256
    cut = a0_ref.shape[1]
    a_copies = {
        first: pltpu.make_async_copy(
            a_hbm.at[:, pl.ds(first, cut)], a1_ref.at[:, pl.ds(first - cut, cut)], sems.at[1 + first // cut]
        )
        for first in range(cut, leaf, cut)
    }
    rank_copy = pltpu.make_async_copy(rank_hbm, rank_ref, sems.at[0])
    u_copy = pltpu.make_async_copy(u_hbm, u_ref, sems.at[1])
    for copy in [rank_copy] + list(a_copies.values()) + [u_copy]:
        copy.start()

    lane = lax.broadcasted_iota(jnp.int32, (LANES, LANES), 1)
    zero = jnp.zeros((LANES, LANES), BF16)

    def build(group):
        def spread(j):
            at = group * 8 + j
            return jnp.broadcast_to(cols_ref[:, at : at + 1], (LANES, LANES))

        both = spread(0).astype(jnp.int32)
        index = [
            jnp.bitwise_and(both, NOWHERE),
            lax.shift_right_logical(both, NOWHERE_BITS),
            spread(1).astype(jnp.int32),
        ]
        index = [i.astype(jnp.int16) for i in index]
        high, low = [], []
        for j in range(3):
            weight = spread(2 + j)
            high.append(weight.astype(BF16))
            low.append(((weight - high[j].astype(F32)) * LOW_SCALE).astype(BF16))
        rows = slice(group * LANES, (group + 1) * LANES)
        for first in range(0, width, LANES):
            place = (lane + first).astype(jnp.int16)
            s_high, s_low = zero, zero
            for j in range(3):
                here = index[j] == place
                s_high = jnp.where(here, high[j], s_high)
                s_low = jnp.where(here, low[j], s_low)
            sh_ref[rows, first : first + LANES] = s_high
            s8_ref[rows, first : first + LANES] = s_low.astype(F8)

    for at in range(0, leaf, piece):
        if at < cut:
            ref, first = a0_ref, at
        else:
            ref, first = a1_ref, at - cut
        if at in a_copies:
            a_copies[at].wait()
        block = slice(first, first + piece)
        w = dot(v_split[:ranks, :], ref[:, block])
        build(2 * (at // piece))
        w = w + dot(v_split[ranks:, :], ref[:, block])
        build(2 * (at // piece) + 1)
        high, low = split(w)
        w_ref[:ranks, at : at + piece] = high
        w_ref[ranks:, at : at + piece] = low
    rank_copy.wait()
    u_copy.wait()
    for level in range(levels):
        rows = slice(level * rank_k, (level + 1) * rank_k)
        u_ref[rows, :] = masked_level(u_ref, rank_ref, level, rank_k)
    high, low = split(u_ref[...])
    part = dot_nt(v_split[...], high)
    part = part[:ranks] + part[ranks:] + dot_nt(v_split[:ranks, :], low)
    for position, level in enumerate(range(levels - 2, -1, -1)):
        h_ref[:, position * rank_k : (position + 1) * rank_k] = part[
            :, level * rank_k : (level + 1) * rank_k
        ]
    used = (levels - 1) * rank_k
    if used < h_ref.shape[1]:
        h_ref[:, used:] = jnp.zeros((ranks, h_ref.shape[1] - used), F32)
    for first in range(0, u_ref.shape[1], piece):
        rows = slice(first, first + piece)
        high, low = split(u_ref[:, rows].T)
        left_ref[rows, :ranks] = high
        left_ref[rows, ranks:] = low


def projections(
    device_ref,
    w_ref,
    sh_ref,
    s8_ref,
    modes_ref,
    inner_ref,
    outer_ref,
    h_ref,
    keep_ref,
    send_ref,
    m_ref,
    m8_ref,
    w8_scr,
    w8_low,
    ws_scr,
    p_scr,
):
    ranks = keep_ref.shape[0]
    own = modes_ref.shape[0]
    half = modes_ref.shape[1] // 2
    m_ref[:own, :] = modes_ref[...]
    core = jnp.bitwise_and(device_ref[0], 1)
    m_ref[pl.ds(pl.multiple_of(own + HALO - core * HALO, HALO), HALO), :] = inner_ref[...]
    m_ref[pl.ds(pl.multiple_of(own + core * HALO, HALO), HALO), :] = outer_ref[...]
    m8_ref[...] = m_ref[...].astype(F8)
    piece = 256
    pieces = [slice(first, first + piece) for first in range(0, sh_ref.shape[1], piece)]

    def main_part(cols):
        return dot(w_ref[:ranks, :], sh_ref[:, cols])

    parts = [main_part(pieces[0])]
    largest = jnp.max(jnp.abs(w_ref[:ranks, :].astype(F32)), axis=1, keepdims=True)
    largest = jnp.maximum(largest, TINY)
    parts.append(main_part(pieces[1]))
    w8_scr[...] = (w_ref[:ranks, :].astype(F32) * (W8_TOP / largest)).astype(F8)
    w8_low[...] = (w_ref[ranks:, :].astype(F32) * (W8_TOP * W_LOW / largest)).astype(F8)
    w_back = largest * (1.0 / (W8_TOP * LOW_SCALE))
    for i, cols in enumerate(pieces):
        if i + 2 < len(pieces):
            parts.append(main_part(pieces[i + 2]))
        top = (sh_ref[:, cols] * jnp.asarray(LOW_SCALE / W_LOW, BF16)).astype(F8)
        part = dot(w8_scr[...], s8_ref[:, cols]) + dot(w8_low[...], top)
        part = parts[i] + part * w_back
        high, low = split(part)
        ws_scr[:ranks, cols] = high
        ws_scr[ranks:, cols] = low
    for first in range(0, 2 * half, piece):
        cols = slice(first, first + piece)
        part = dot(ws_scr[...], m_ref[:, cols])
        p_scr[:, cols] = part[:ranks] + part[ranks:]
    mine = pl.multiple_of(core * half, half)
    other = pl.multiple_of((1 - core) * half, half)
    keep_ref[:, :half] = p_scr[:, pl.ds(mine, half)]
    send_ref[:, :half] = p_scr[:, pl.ds(other, half)]
    keep_ref[:, half:] = h_ref[...]
    send_ref[:, half:] = h_ref[...]


def chunks(rows, lanes, width):
    across = width // LANES
    places = [(r, c) for c in range(0, lanes, LANES) for r in range(0, rows, 16)]
    return [((t // across * 16, t % across * LANES), place) for t, place in enumerate(places)]


def chunk_rows(rows, lanes, width):
    return 16 * -(-(rows // 16) * (lanes // LANES) // (width // LANES))


def stage(device_ref, core_ref, mine_ref, other_ref, *refs, level, levels, rank_k, half):
    side = jnp.bitwise_and(lax.shift_right_logical(device_ref[0], level), 1)
    upper = jnp.full((rank_k, half), side, jnp.int32) == 1
    mine = mine_ref[:rank_k, :half]
    other = other_ref[:rank_k, :half].astype(F32)
    stack = jnp.concatenate([jnp.where(upper, other, mine), jnp.where(upper, mine, other)], axis=0)
    coef = dot_split(core_ref[level], stack)
    c_mine = jnp.where(upper, coef[:rank_k], coef[rank_k:])
    c_other = jnp.where(upper, coef[rank_k:], coef[:rank_k])
    if level < levels - 1:
        next_ref, send_ref, c_ref = refs[0], refs[1], refs[2]
        at = (levels - 2 - level) * rank_k
        rows = mine_ref.shape[0]
        if level == 0:
            h_all = other_ref[rank_k:, half:]
        else:
            columns = {}
            for (r, c), (_, column) in chunks(rows - rank_k, mine_ref.shape[1] - half, half):
                piece = other_ref[rows + r : rows + r + 16, c : c + LANES]
                columns.setdefault(column, []).append(piece)
            columns = [jnp.concatenate(columns[c], axis=0) for c in sorted(columns)]
            h_all = jnp.concatenate(columns, axis=1).astype(F32)
        h_mine = mine_ref[rank_k:, half + at : half + at + rank_k]
        h_other = h_all[:, at : at + rank_k]
        q = mine_ref[rank_k:, :half] + other_ref[rank_k:rows, :half].astype(F32)
        q = q - dot_split(h_mine, c_mine) - dot_split(h_other, c_other)
        next_ref[:, :half] = q
        after_rows, end = next_ref.shape
        send_ref[:after_rows, :] = q.astype(send_ref.dtype)
        if end > half:
            h = mine_ref[rank_k:, half:end] + h_all[:, : end - half]
            next_ref[:, half:] = h
            packed = h[rank_k:].astype(send_ref.dtype)
            for (r, c), (row, column) in chunks(after_rows - rank_k, end - half, half):
                piece = packed[row : row + 16, column : column + LANES]
                send_ref[after_rows + r : after_rows + r + 16, c : c + LANES] = piece
            filled = (after_rows - rank_k) // 16 * ((end - half) // LANES) % (half // LANES)
            if filled:
                rest = send_ref.shape[0] - 16
                blank = jnp.zeros((16, half - filled * LANES), send_ref.dtype)
                send_ref[rest:, filled * LANES :] = blank
        c_ref[0] = c_mine
        if level == 0:
            c_ref[1] = c_other
    else:
        before, keep_ref, send_ref = refs[: levels - 1], refs[-2], refs[-1]
        for ref_level, ref in enumerate(before):
            rows = slice(ref_level * rank_k, (ref_level + 1) * rank_k)
            keep_ref[rows, :] = ref[0]
            send_ref[rows, :] = ref[1] if ref_level == 0 else ref[0]
        rows = slice(level * rank_k, (level + 1) * rank_k)
        keep_ref[rows, :] = c_mine
        send_ref[rows, :] = c_other if level == 0 else c_mine


def interpolate(sh_ref, s8_ref, m_ref, m8_ref, t_ref, *, start):
    block, piece = 512, 256
    for row in range(0, t_ref.shape[0], block):
        rows = slice(start + row, start + row + block)
        for first in range(0, t_ref.shape[1], piece):
            cols = slice(first, first + piece)
            part = dot(sh_ref[rows, :], m_ref[:, cols])
            part = part + dot(s8_ref[rows, :], m8_ref[:, cols]) * (1.0 / LOW_SCALE)
            t_ref[row : row + block, cols] = part.astype(BF16)


def leaf_solve(a0_ref, a1_ref, t0_ref, t1_ref, y_ref, *, start):
    block, piece = 512, 256
    for row in range(0, y_ref.shape[0], block):
        rows = slice(start + row, start + row + block)
        for first in range(0, y_ref.shape[1], piece):
            cols = slice(first, first + piece)
            part = dot(a0_ref[rows, :], t0_ref[:, cols]) + dot(a1_ref[rows, :], t1_ref[:, cols])
            y_ref[row : row + block, cols] = part


def update(device_ref, left_ref, y0_ref, y1_ref, c_ref, *refs, own_half):
    out_ref, c_scr, o_scr, sems = refs[-4:]
    ranks, half = c_ref.shape
    core = jnp.bitwise_and(device_ref[0], 1)
    at = pl.multiple_of((core if own_half else 1 - core) * half, half)
    high, low = split(c_ref[...])
    c_scr[:ranks, :] = high
    c_scr[ranks : 2 * ranks, :] = high
    c_scr[2 * ranks :, :] = low
    block, piece = 256, 256
    copies = []
    for row in range(0, o_scr.shape[0], block):
        rows = slice(row, row + block)
        if row < y0_ref.shape[0]:
            ref, begin = y0_ref, row
        else:
            ref, begin = y1_ref, row - y0_ref.shape[0]
        for first in range(0, half, piece):
            cols = slice(first, first + piece)
            part = dot(left_ref[rows, :], c_scr[: 2 * ranks, cols])
            part = part + dot(left_ref[rows, :ranks], c_scr[2 * ranks :, cols])
            solved = ref[begin : begin + block, pl.ds(pl.multiple_of(at + first, piece), piece)]
            o_scr[rows, cols] = solved - part
        copy = pltpu.make_async_copy(
            o_scr.at[pl.ds(row, block)],
            out_ref.at[pl.ds(row, block), pl.ds(at, half)],
            sems.at[row // block],
        )
        copy.start()
        copies.append(copy)
    for copy in copies:
        copy.wait()


def local(
    modes,
    node_index,
    interp_weight,
    leaf_order,
    leaf_inverse,
    v_factor,
    u_factor,
    core_table,
    level_rank,
):
    own, rhs = modes.shape
    half = rhs // 2
    levels, rank_k, leaf = v_factor.shape
    ranks = levels * rank_k
    count = lax.axis_size("narrow")
    device = lax.axis_index("narrow").astype(jnp.int32)
    device = device.reshape(1)
    width = own + 2 * HALO
    shape = pltpu.VMEM
    half_rows = leaf // 2
    first_rows = leaf // 4

    def partner(value, bit):
        return lax.ppermute(value, "narrow", [(s, s ^ (1 << bit)) for s in range(count)])

    def after(value, token):
        return lax.optimization_barrier((value, token))[0]

    v_rows = v_factor.reshape(ranks, leaf)
    u_rows = u_factor.reshape(ranks, leaf)

    def h_width(level):
        return ceil_to(rank_k * (levels - 1 - level), LANES)

    groups = leaf // LANES
    inner, outer, columns, cores, v_split, a_left = pl.pallas_call(
        functools.partial(prepare, levels=levels, rank_k=rank_k),
        in_specs=[scalars()] + [anywhere()] * 8,
        out_specs=[whole()] * 6,
        out_shape=[
            shape((HALO, rhs), BF16),
            shape((HALO, rhs), BF16),
            shape((LANES, groups * 8), F32),
            shape((levels, 2 * rank_k, 2 * rank_k), F32),
            shape((2 * ranks, leaf), BF16),
            shape((leaf, first_rows), BF16),
        ],
        scratch_shapes=[
            pltpu.SMEM((levels,), jnp.int32),
            pltpu.VMEM((groups, LANES), jnp.int32),
            pltpu.VMEM((3, leaf), jnp.int32),
            pltpu.VMEM((3, leaf), F32),
            pltpu.VMEM((ranks, leaf), F32),
            pltpu.VMEM((groups * 8, LANES), F32),
            pltpu.SemaphoreType.DMA((8 + levels,)),
        ],
        compiler_params=params(8),
        cost_estimate=cost(1e9, 8e6),
        name="prepare",
    )(
        device,
        in_hbm(level_rank),
        in_hbm(leaf_order.reshape(groups, LANES)),
        in_hbm(node_index),
        in_hbm(interp_weight),
        in_hbm(modes),
        in_hbm(core_table),
        in_hbm(v_rows),
        in_hbm(leaf_inverse),
    )

    rim_inner = partner(inner, 0)
    swaps = [(i, i + 1) for i in range(1, count - 1, 2)]
    rim_outer = lax.ppermute(outer, "narrow", swaps + [(j, i) for i, j in swaps])

    s_high, s_low8, w, h, left, a_right = pl.pallas_call(
        functools.partial(leaf_operators, levels=levels, rank_k=rank_k),
        in_specs=[anywhere(), whole(), whole(), anywhere(), whole(), anywhere()],
        out_specs=[whole()] * 6,
        out_shape=[
            shape((leaf, width), BF16),
            shape((leaf, width), F8),
            shape((2 * ranks, leaf), BF16),
            shape((ranks, h_width(0)), F32),
            shape((leaf, 2 * ranks), BF16),
            shape((leaf, leaf - first_rows), BF16),
        ],
        scratch_shapes=[
            pltpu.SMEM((levels,), jnp.int32),
            pltpu.VMEM((ranks, leaf), F32),
            pltpu.SemaphoreType.DMA((1 + leaf // first_rows,)),
        ],
        compiler_params=params(12),
        cost_estimate=cost(5e9, 14e6),
        name="leaf_operators",
    )(in_hbm(level_rank), columns, v_split, in_hbm(u_rows), a_left, in_hbm(leaf_inverse))

    wide = half + h_width(0)
    mine, send, m, m8 = pl.pallas_call(
        projections,
        in_specs=[scalars()] + [whole()] * 7,
        out_specs=[whole()] * 4,
        out_shape=[
            shape((ranks, wide), F32),
            shape((ranks, wide), F32),
            shape((width, rhs), BF16),
            shape((width, rhs), F8),
        ],
        scratch_shapes=[
            pltpu.VMEM((ranks, leaf), F8),
            pltpu.VMEM((ranks, leaf), F8),
            pltpu.VMEM((2 * ranks, width), BF16),
            pltpu.VMEM((ranks, rhs), F32),
        ],
        compiler_params=params(8),
        cost_estimate=cost(5e9, 14e6),
        name="projections",
    )(device, w, s_high, s_low8, modes, rim_inner, rim_outer, h)

    def run_interpolate(start, size, token):
        return pl.pallas_call(
            functools.partial(interpolate, start=start),
            in_specs=[whole()] * 4,
            out_specs=whole(),
            out_shape=shape((size, rhs), BF16),
            compiler_params=params(4),
            cost_estimate=cost(4e9, 8e6),
            name="interpolate",
        )(s_high, s_low8, m, after(m8, token))

    def run_leaf(t0, t1, start, token):
        return pl.pallas_call(
            functools.partial(leaf_solve, start=start),
            in_specs=[whole()] * 4,
            out_specs=whole(),
            out_shape=shape((half_rows, rhs), F32),
            compiler_params=params(4),
            cost_estimate=cost(4.3e9, 10e6),
            name="leaf_solve",
        )(a_left, a_right, t0, after(t1, token))

    def run_stage(level, mine, other, before):
        if level == levels - 1:
            out_shape = [shape((ranks, half), F32)] * 2
            extra = before
        else:
            size = (mine.shape[0] - rank_k, half + h_width(level + 1))
            out_shape = [
                shape(size, F32),
                shape((size[0] + chunk_rows(size[0] - rank_k, size[1] - half, half), half), BF16),
                shape((2 if level == 0 else 1, rank_k, half), F32),
            ]
            extra = []
        return pl.pallas_call(
            functools.partial(stage, level=level, levels=levels, rank_k=rank_k, half=half),
            in_specs=[scalars()] + [whole()] * (3 + len(extra)),
            out_specs=[whole()] * len(out_shape),
            out_shape=out_shape,
            compiler_params=params(6),
            cost_estimate=cost(1e8, 1e6),
            name="stage",
        )(device, cores, mine, other, *extra)

    parts = {}

    def beside(position, token):
        if position == 0:
            parts["t0"] = run_interpolate(0, first_rows, token)
            return parts["t0"]
        if position == 1:
            parts["t1"] = run_interpolate(first_rows, leaf - first_rows, token)
            return parts["t1"]
        if position == 2:
            parts["y0"] = run_leaf(parts["t0"], parts["t1"], 0, token)
            return parts["y0"]
        if position == 3:
            parts["y1"] = run_leaf(parts["t0"], parts["t1"], half_rows, token)
            return parts["y1"]
        return None

    before = []
    for level in range(levels):
        other = partner(send, level)
        token = beside(level, send)
        if token is not None:
            mine = after(mine, token)
        got = run_stage(level, mine, other, before)
        if level < levels - 1:
            mine, send = got[0], got[1]
            before.append(got[2])
    keep, send = got
    crossed = partner(send, 0)

    def run_update(c, before, own_half):
        return pl.pallas_call(
            functools.partial(update, own_half=own_half),
            in_specs=[scalars()] + [whole()] * 4 + [anywhere()] * len(before),
            out_specs=anywhere(),
            out_shape=pltpu.HBM((leaf, rhs), F32),
            input_output_aliases={5: 0} if before else {},
            scratch_shapes=[
                pltpu.VMEM((3 * ranks, half), BF16),
                pltpu.VMEM((leaf, half), F32),
                pltpu.SemaphoreType.DMA((leaf // 256,)),
            ],
            compiler_params=params(10),
            cost_estimate=cost(1.7e9, 9e6),
            name="update",
        )(device, left, parts["y0"], parts["y1"], c, *before)

    out = run_update(after(keep, send), [], True)
    return run_update(crossed, [out], False)


def solution(mesh):
    in_specs = (
        P(("groups", "narrow"), None),
        P(None, ("groups", "narrow")),
        P(None, ("groups", "narrow")),
        P(("groups", "narrow")),
        P(("groups", "narrow"), None),
        P(None, None, ("groups", "narrow")),
        P(None, None, ("groups", "narrow")),
        P("groups", None, None),
        P("groups"),
    )
    out_specs = P(("groups", "narrow"), None)
    return jax.shard_map(local, mesh=mesh, in_specs=in_specs, out_specs=out_specs, check_vma=False)
```
